256 devices in a mesh: row: 32 (over x, y, core), col: 8 (over z).
Axes of the slice: x: 4, y: 4, z: 8, core: 2. Of those that a mesh axis runs over, the one named last changes fastest.
Arguments:
- inputs: float32 [512, 12288], P('row', 'col'), may hold values from -600 to 600, as said below
- gain: float32 [12288], P('col'), may hold values from 0.1 to 1.9
- bias: float32 [12288], P('col'), may hold values from -3 to 3
- weight: bfloat16 [12288, 49152], P('col', 'row'), may hold values from -0.0546875 to 0.0546875
- d_act: bfloat16 [512, 49152], P('col', 'row'), may hold values from -1.5 to 1.5
Outputs:
- activated: bfloat16 [512, 49152], P('col', 'row')
- d_normed: bfloat16 [512, 12288], P('row', 'col')
- d_weight: bfloat16 [12288, 49152], P('col', 'row')
The draws below stay inside these ranges and needn't reach their ends.
Inputs may be any that keep to these rules, and one draw needn't show every extreme that they name: `inputs`: finite values.
All inputs are finite; a program needn't handle non-finite values.
Results may differ from the reference program's by a relative error of at most 0.024.
Values may be sent and summed in bfloat16 or wider, within the bound.
No kernel may reach another device: no remote copies, remote signals or barrier semaphores. Data moves between devices by JAX's collectives and lax.ppermute only.
A program may use at most 64 MiB of HBM per device.

```python
import jax
import jax.numpy as jnp
from jax import lax

D = 12288
FF = 49152
TOKENS = 512


def draw_inputs(key, part):
    key = jax.random.fold_in(key, 11)
    key_rows, key_cols, key_base, key_pick, key_sign, key_level = jax.random.split(key, 6)
    row_scale = jnp.exp(jax.random.uniform(key_rows, (TOKENS, 1), jnp.float32) * jnp.log(10.0))
    position = jnp.arange(D, dtype=jnp.float32)[None, :] / D
    ramp = 1.0 + 2.0 * position
    col_scale = ramp * jnp.exp(jax.random.uniform(key_cols, (1, D), jnp.float32) * jnp.log(3.0))
    level = jax.random.uniform(key_level, (TOKENS, 1), jnp.float32, 1.0, 2.0)
    level = level * jnp.where(jax.random.uniform(key_level, (TOKENS, 1), jnp.float32) < 0.5, -1.0, 1.0)
    base = jnp.clip(jax.random.normal(key_base, (TOKENS, D), jnp.float32), -6.0, 6.0)
    profile = 1.0 + 2.0 * position
    picked = jax.random.uniform(key_pick, (TOKENS, 1), jnp.float32) < 0.25
    signs = jnp.where(jax.random.uniform(key_sign, (TOKENS, 1), jnp.float32) < 0.5, -1.0, 1.0)
    shifted = 250.0 * signs + 0.01 * base * col_scale
    drawn = row_scale * (base * col_scale + level * profile)
    return jnp.clip(jnp.where(picked, shifted, drawn), -590.0, 590.0).astype(jnp.float32)


def raised(entries, stream_key, source, target, parts, factor):
    def block_of(axis_at):
        return (jnp.arange(entries.shape[axis_at]) // (entries.shape[axis_at] // parts)).reshape((-1,) + (1,) * (entries.ndim - 1 - axis_at))

    first = jax.random.permutation(stream_key, parts)[block_of(target)]
    far = (block_of(target) + parts // 2) % parts
    return jnp.where((block_of(source) == first) | (block_of(source) == far), factor * entries, entries)


def levels(rng, shape, cuts, smallest, high):
    loudness = 1.0
    for dim, shards_of in cuts:
        steps = jax.random.uniform(jax.random.fold_in(jax.random.fold_in(rng, 6), dim), (shards_of,), jnp.float32, smallest / len(cuts), high / len(cuts))
        loudness = loudness * jnp.repeat(jnp.exp(steps), shape[dim] // shards_of).reshape((-1,) + (1,) * (len(shape) - 1 - dim))
    return loudness


def normal_values(rng, dims, scale, limit, cuts=(), kind=jnp.bfloat16):
    level = levels(rng, dims, cuts, -0.22, 0.18) if cuts else 1.0
    entries = jax.random.normal(rng, dims, jnp.float32) * scale * level
    return jnp.minimum(jnp.maximum(entries, -limit), limit).astype(kind)


def heavy_noise(own_key, dims, deviation, limit, cuts, heavy, kind=jnp.bfloat16):
    values = deviation * jax.random.normal(own_key, dims, jnp.float32)
    if cuts:
        values = values * levels(own_key, dims, cuts, -0.22, 0.18)
    return jnp.clip(raised(values, jax.random.fold_in(own_key, 3), *heavy), -limit, limit).astype(kind)


def setup_inputs(seed: int = 0) -> dict:
    streams_of = jax.random.split(jax.random.key(seed), 6)
    inputs = draw_inputs(jax.random.fold_in(streams_of[5], 71), 0)
    gain = jnp.clip(1.0 + 0.18 * jax.random.normal(streams_of[1], (D,), jnp.float32), 0.1, 1.9)
    bias = normal_values(streams_of[2], (D,), 0.5, 3.0, ((0, 8),), jnp.float32)
    weight = normal_values(streams_of[3], (D, FF), D ** -0.5, 0.0546875, ((0, 8), (1, 32)))
    d_act = heavy_noise(streams_of[4], (TOKENS, FF), 0.25, 1.5, ((0, 8), (1, 32)), (1, 0, 32, 2.75))
    return dict(inputs=inputs, gain=gain, bias=bias, weight=weight, d_act=d_act)


def gelu_tanh(value):
    return jax.nn.gelu(value, approximate=True)

def reference(inputs, gain, bias, weight, d_act):
    values = inputs.astype(jnp.float32)
    row_mean = lax.optimization_barrier(jnp.mean(values, axis=1, keepdims=True))
    centered = values - row_mean
    spread = lax.optimization_barrier(jnp.mean(centered * centered, axis=1, keepdims=True))
    normed = (centered * lax.rsqrt(spread + 1e-05) * gain[None, :] + bias[None, :]).astype(jnp.bfloat16)
    pre = jnp.dot(normed, weight, preferred_element_type=jnp.float32)
    result, pullback = jax.vjp(gelu_tanh, pre)
    activated = result.astype(jnp.bfloat16)
    d_pre = pullback(d_act.astype(jnp.float32))[0].astype(jnp.bfloat16)
    block_width = FF // 8
    pieces = []
    for start_col in range(0, FF, block_width):
        pieces.append(jnp.dot(normed.T, d_pre[:, start_col:start_col + block_width], preferred_element_type=jnp.float32).astype(jnp.bfloat16))
    d_weight = jnp.concatenate(pieces, axis=1)
    d_normed = jnp.dot(d_pre, weight.T, preferred_element_type=jnp.float32).astype(jnp.bfloat16)
    return (activated, d_normed, d_weight)
```

```python
import functools

import jax
import jax.numpy as jnp
from jax import lax
from jax.experimental import pallas as pl
from jax.experimental.pallas import tpu as pltpu
from jax.sharding import PartitionSpec as P

D = 12288
F32, BF16 = jnp.float32, jnp.bfloat16

NX, NY, NC, NZ = 4, 4, 2, 8
SHIFT = (0, 1, 3, 2)
TOKENS_OWN = 16
TOKENS_Z = 64
TOKENS = 512


def row_pairs(dx, dy, dc):
    pairs = []
    for x in range(NX):
        for y in range(NY):
            for c in range(NC):
                source = (x * NY + y) * NC + c
                target = (((x + dx) % NX) * NY + (y + dy) % NY) * NC + (c + dc) % NC
                pairs.append((source, target))
    return pairs


def send_row(value, dx=0, dy=0, dc=0):
    return lax.ppermute(value, "row", row_pairs(dx, dy, dc))


def send_col(value, dz):
    return lax.ppermute(value, "col", [(z, (z + dz) % NZ) for z in range(NZ)])


def token_offset(core_shift, x_shift, y_shift):
    row, col = lax.axis_index("row"), lax.axis_index("col")
    x, y, c = row // (NY * NC), (row // NC) % NY, row % NC
    block = (((x + x_shift) % NX) * NY + (y + y_shift) % NY) * NC + (c + core_shift) % NC
    offset = (block * TOKENS_OWN - col * TOKENS_Z + TOKENS) % TOKENS
    return pl.multiple_of(offset, TOKENS_OWN)


def first_kernel(*refs):
    pieces, (w_ref, normed_ref), outs = refs[:8], refs[8:10], refs[10:]

    @pl.when(pl.program_id(0) == 0)
    def _():
        for core_shift in range(2):
            for iy in range(4):
                for ix in range(4):
                    offset = token_offset(core_shift, NX - SHIFT[ix], NY - SHIFT[iy])
                    normed_ref[pl.ds(offset, TOKENS_OWN), :] = pieces[core_shift * 4 + iy][
                        ix * TOKENS_OWN : (ix + 1) * TOKENS_OWN, :
                    ]

    product = jnp.dot(normed_ref[...], w_ref[...], preferred_element_type=F32)
    for k in range(NZ):
        outs[k][...] = product[k * TOKENS_Z : (k + 1) * TOKENS_Z, :].astype(outs[k].dtype)


def second_kernel(normed_ref, w_ref, *outs):
    product = jnp.dot(normed_ref[...], w_ref[...], preferred_element_type=F32)
    for k in range(NZ):
        outs[k][...] = product[k * TOKENS_Z : (k + 1) * TOKENS_Z, :].astype(outs[k].dtype)


def partial_pre(kernel, operands, weight, half, tile, first):
    depth, width = weight.shape
    steps = width // 2 // tile
    outs = [jax.ShapeDtypeStruct((TOKENS_Z, width // 2), BF16)] * NZ
    out_specs = [pl.BlockSpec((TOKENS_Z, tile), lambda j: (0, j))] * NZ
    if first:
        outs = [jax.ShapeDtypeStruct((TOKENS, depth), BF16)] + outs
        out_specs = [pl.BlockSpec((TOKENS, depth), lambda j: (0, 0))] + out_specs
    return pl.pallas_call(
        kernel,
        grid=(steps,),
        in_specs=[pl.BlockSpec(v.shape, lambda j: (0, 0)) for v in operands]
        + [pl.BlockSpec((depth, tile), lambda j: (0, j + half * steps))],
        out_specs=out_specs,
        out_shape=outs,
        compiler_params=pltpu.CompilerParams(vmem_limit_bytes=24 << 20),
        cost_estimate=pl.CostEstimate(
            flops=TOKENS * depth * width, bytes_accessed=depth * width * 2, transcendentals=0
        ),
    )(*operands, weight)


def third_kernel(*refs):
    pieces, w_ref, slopes_ref, outs, acc = refs[:16], refs[16], refs[17], refs[18:26], refs[26]
    half = slopes_ref.shape[1] // 2

    @pl.when(pl.program_id(0) == 0)
    def _():
        for k in range(NZ):
            for h in range(2):
                slopes_ref[
                    k * TOKENS_Z : (k + 1) * TOKENS_Z, h * half : (h + 1) * half
                ] = pieces[h * 8 + k][...]

    acc[...] = lax.dot_general(
        slopes_ref[...], w_ref[...], (((1,), (1,)), ((), ())), preferred_element_type=F32
    )
    for core_shift in range(2):
        for iy in range(4):
            for ix in range(4):
                offset = token_offset(core_shift, SHIFT[ix], SHIFT[iy])
                outs[core_shift * 4 + iy][ix * TOKENS_OWN : (ix + 1) * TOKENS_OWN, :] = acc[
                    pl.ds(offset, TOKENS_OWN), :
                ].astype(BF16)


def partial_normed(pieces, weight, tile):
    depth, width = weight.shape
    return pl.pallas_call(
        third_kernel,
        grid=(depth // tile,),
        in_specs=[pl.BlockSpec(v.shape, lambda j: (0, 0)) for v in pieces]
        + [pl.BlockSpec((tile, width), lambda j: (j, 0))],
        out_specs=[pl.BlockSpec((TOKENS, width), lambda j: (0, 0))]
        + [pl.BlockSpec((TOKENS_Z, tile), lambda j: (0, j))] * 8,
        out_shape=[jax.ShapeDtypeStruct((TOKENS, width), BF16)]
        + [jax.ShapeDtypeStruct((TOKENS_Z, depth), BF16)] * 8,
        scratch_shapes=[pltpu.VMEM((TOKENS, tile), F32)],
        compiler_params=pltpu.CompilerParams(vmem_limit_bytes=24 << 20),
        cost_estimate=pl.CostEstimate(
            flops=2 * TOKENS * depth * width, bytes_accessed=depth * width * 2, transcendentals=0
        ),
    )(*pieces, weight)


def gelu_tanh(value):
    return jax.nn.gelu(value, approximate=True)


def add(*values):
    total = values[0].astype(F32)
    for value in values[1:]:
        total = total + value.astype(F32)
    return total


def reduce_chain(parts, dz):
    travelling = send_col(parts[0], dz)
    for part in parts[1:]:
        travelling = send_col(add(part, travelling).astype(BF16), dz)
    return travelling


def gather_chain(own, dz, count):
    got = []
    for _ in range(count):
        own = send_col(own, dz)
        got.append(own)
    return got


def normalize(inputs, gain, bias):
    local = inputs.shape[1]
    local_mean = jnp.sum(inputs, axis=1) / local
    centered = inputs - local_mean[:, None]
    local_square = jnp.sum(centered * centered, axis=1)
    stats = jnp.stack([local_mean, local_square])
    every = jnp.stack([stats] + [send_col(stats, dz) for dz in (1, 7, 2, 6, 3, 5, 4)])
    mean = jnp.mean(every[:, 0, :], axis=0)
    offset = every[:, 0, :] - mean[None, :]
    spread = (jnp.sum(every[:, 1, :], axis=0) + local * jnp.sum(offset * offset, axis=0)) / D
    scale = lax.rsqrt(spread + 1e-05)
    moved = centered + (local_mean - mean)[:, None]
    return (moved * scale[:, None] * gain[None, :] + bias[None, :]).astype(BF16)


def per_device(inputs, gain, bias, weight, d_act):
    half = weight.shape[1] // 2
    normed = normalize(inputs, gain, bias)

    along_x = jnp.concatenate([normed] + [send_row(normed, dx=s) for s in SHIFT[1:]])
    along_y = [along_x] + [send_row(along_x, dy=s) for s in SHIFT[1:]]
    other = [send_row(v, dc=1) for v in along_y]

    gathered, *parts_a = partial_pre(first_kernel, along_y + other, weight, 0, 384, True)
    parts_b = partial_pre(second_kernel, [gathered], weight, 1, 384, False)

    a_right = reduce_chain([parts_a[k] for k in (4, 3, 2, 1)], 1)
    a_left = reduce_chain([parts_a[k] for k in (5, 6, 7)], -1)
    b_right = reduce_chain([parts_b[k] for k in (3, 2, 1)], 1)
    b_left = reduce_chain([parts_b[k] for k in (4, 5, 6, 7)], -1)

    activated, slopes = [], []
    for h, total in enumerate((add(parts_a[0], a_right, a_left), add(parts_b[0], b_right, b_left))):
        result, pullback = jax.vjp(gelu_tanh, total)
        activated.append(result.astype(BF16))
        cotangent = d_act[:, h * half : (h + 1) * half].astype(F32)
        slopes.append(pullback(cotangent)[0].astype(BF16))
    a_back = gather_chain(slopes[0], 1, 4)
    a_ahead = gather_chain(slopes[0], -1, 3)
    b_back = gather_chain(slopes[1], 1, 3)
    b_ahead = gather_chain(slopes[1], -1, 4)
    pieces = [slopes[0]] + a_ahead + a_back[::-1] + [slopes[1]] + b_ahead + b_back[::-1]

    slopes_all, *parts = partial_normed(pieces, weight, 512)
    d_weight = lax.dot_general(
        gathered, slopes_all, (((0,), (0,)), ((), ())), preferred_element_type=F32
    ).astype(BF16)

    sums = [add(parts[i], send_row(parts[4 + i], dc=1)) for i in range(4)]
    arrived = [send_row(sums[i].astype(BF16), dy=SHIFT[i]) for i in range(1, 4)]
    column = add(sums[0], *arrived)
    blocks = [column[i * TOKENS_OWN : (i + 1) * TOKENS_OWN] for i in range(4)]
    arrived = [send_row(blocks[i].astype(BF16), dx=SHIFT[i]) for i in range(1, 4)]
    d_normed = add(blocks[0], *arrived).astype(BF16)
    return (jnp.concatenate(activated, axis=1), d_normed, d_weight)


def solution(mesh):
    return jax.shard_map(
        per_device,
        mesh=mesh,
        in_specs=(P("row", "col"), P("col"), P("col"), P("col", "row"), P("col", "row")),
        out_specs=(P("col", "row"), P("row", "col"), P("col", "row")),
        check_vma=False,
    )
```

```python
import functools

import jax
import jax.numpy as jnp
from jax import lax
from jax.experimental import pallas as pl
from jax.experimental.pallas import tpu as pltpu
from jax.sharding import Mesh
from jax.sharding import PartitionSpec as P

D = 12288
F32, BF16 = jnp.float32, jnp.bfloat16

NX, NY, NC, NZ = 4, 4, 2, 8
CHIPS = NX * NY
OWN = 16
TOKENS_Z = 64
TOKENS = 512
BACKWARD = [list(range(NZ))[::-1]]

VMEM = pl.BlockSpec(memory_space=pltpu.VMEM)
HBM = pl.BlockSpec(memory_space=pltpu.HBM)


def fetch(source, held, sems, steps, piece):
    copies = [
        pltpu.make_async_copy(source.at[piece(i)], held.at[i], sems.at[i]) for i in range(steps)
    ]
    for copy in copies:
        copy.start()
    return copies


def token_offset(chip, core_shift):
    core = (lax.axis_index("core") + core_shift) % NC
    return pl.multiple_of((chip * NC + core) * OWN, OWN)


def z_rows(k, reverse):
    k = NZ - 1 - k if reverse else k
    return slice(k * TOKENS_Z, (k + 1) * TOKENS_Z)


def multiply(steps, tile, copies, normed_ref, held, out_ref, reverse):
    for i in range(steps):
        copies[i].wait()
        product = jnp.dot(normed_ref[...], held[i], preferred_element_type=F32).astype(BF16)
        for k in range(NZ):
            out_ref[z_rows(k, reverse), i * tile : (i + 1) * tile] = product[z_rows(k, False), :]


def first_kernel(steps, tile, base, own_ref, other_ref, w_ref, normed_ref, out_ref, held, sems):
    copies = fetch(w_ref, held, sems, steps, lambda i: (slice(None), pl.ds(base + i * tile, tile)))
    for core_shift, piece in enumerate((own_ref, other_ref)):
        for chip in range(CHIPS):
            normed_ref[pl.ds(token_offset(chip, core_shift), OWN), :] = piece[
                chip * OWN : (chip + 1) * OWN, :
            ]
    multiply(steps, tile, copies, normed_ref, held, out_ref, False)


def second_kernel(steps, tile, base, normed_ref, w_ref, out_ref, held, sems):
    copies = fetch(w_ref, held, sems, steps, lambda i: (slice(None), pl.ds(base + i * tile, tile)))
    multiply(steps, tile, copies, normed_ref, held, out_ref, True)


def partial_pre(kernel, operands, weight, half, tile, first):
    depth, width = weight.shape
    steps = width // 2 // tile
    outs = [jax.ShapeDtypeStruct((TOKENS, width // 2), BF16)]
    if first:
        outs = [jax.ShapeDtypeStruct((TOKENS, depth), BF16)] + outs
    return pl.pallas_call(
        functools.partial(kernel, steps, tile, half * width // 2),
        in_specs=[VMEM] * len(operands) + [HBM],
        out_specs=[VMEM] * len(outs),
        out_shape=outs,
        scratch_shapes=[pltpu.VMEM((steps, depth, tile), BF16), pltpu.SemaphoreType.DMA((steps,))],
        compiler_params=pltpu.CompilerParams(vmem_limit_bytes=24 << 20),
        cost_estimate=pl.CostEstimate(
            flops=TOKENS * depth * width, bytes_accessed=depth * width * 2, transcendentals=0
        ),
    )(*operands, weight)


def third_kernel(steps, tile, a_ref, b_ref, w_ref, slopes_ref, own_ref, other_ref, held, acc, sems):
    half = slopes_ref.shape[1] // 2
    copies = fetch(w_ref, held, sems, steps, lambda i: (pl.ds(i * tile, tile), slice(None)))
    slopes_ref[:, :half] = a_ref[...]
    for k in range(NZ):
        slopes_ref[z_rows(k, False), half:] = b_ref[z_rows(k, True), :]
    for step in range(steps):
        copies[step].wait()
        acc[...] = lax.dot_general(
            slopes_ref[...], held[step], (((1,), (1,)), ((), ())), preferred_element_type=F32
        )
        columns = slice(step * tile, (step + 1) * tile)
        for core_shift, piece in enumerate((own_ref, other_ref)):
            for chip in range(CHIPS):
                piece[chip * OWN : (chip + 1) * OWN, columns] = acc[
                    pl.ds(token_offset(chip, core_shift), OWN), :
                ].astype(BF16)


def partial_normed(slopes_a, slopes_b, weight, tile):
    depth, width = weight.shape
    steps = depth // tile
    return pl.pallas_call(
        functools.partial(third_kernel, steps, tile),
        in_specs=[VMEM, VMEM, HBM],
        out_specs=[VMEM] * 3,
        out_shape=[
            jax.ShapeDtypeStruct((TOKENS, width), BF16),
            jax.ShapeDtypeStruct((TOKENS // 2, depth), BF16),
            jax.ShapeDtypeStruct((TOKENS // 2, depth), BF16),
        ],
        scratch_shapes=[
            pltpu.VMEM((steps, tile, width), BF16),
            pltpu.VMEM((TOKENS, tile), F32),
            pltpu.SemaphoreType.DMA((steps,)),
        ],
        compiler_params=pltpu.CompilerParams(vmem_limit_bytes=24 << 20),
        cost_estimate=pl.CostEstimate(
            flops=2 * TOKENS * depth * width, bytes_accessed=depth * width * 2, transcendentals=0
        ),
    )(slopes_a, slopes_b, weight)


def gelu_tanh(value):
    return jax.nn.gelu(value, approximate=True)


def send_core(value):
    return lax.ppermute(value, "core", [(0, 1), (1, 0)])


def normalize(inputs, gain, bias):
    local = inputs.shape[1]
    local_mean = jnp.sum(inputs, axis=1) / local
    centered = inputs - local_mean[:, None]
    local_square = jnp.sum(centered * centered, axis=1)
    stats = jnp.stack([local_mean, local_square])
    every = lax.all_to_all(jnp.broadcast_to(stats[None], (NZ,) + stats.shape), "col", 0, 0)
    mean = jnp.mean(every[:, 0, :], axis=0)
    offset = every[:, 0, :] - mean[None, :]
    spread = (jnp.sum(every[:, 1, :], axis=0) + local * jnp.sum(offset * offset, axis=0)) / D
    scale = lax.rsqrt(spread + 1e-05)
    moved = centered + (local_mean - mean)[:, None]
    return (moved * scale[:, None] * gain[None, :] + bias[None, :]).astype(BF16)


def per_device(inputs, gain, bias, weight, d_act):
    half = weight.shape[1] // 2
    depth = weight.shape[0]
    normed = normalize(inputs, gain, bias)

    copies = jnp.broadcast_to(normed[None], (CHIPS, OWN, depth))
    plane = lax.all_to_all(copies, ("x", "y"), 0, 0).reshape(CHIPS * OWN, depth)
    other = send_core(plane)

    gathered, part_a = partial_pre(first_kernel, [plane, other], weight, 0, 256, True)
    (part_b,) = partial_pre(second_kernel, [gathered], weight, 1, 256, False)
    total_a = lax.psum_scatter(part_a, "col", scatter_dimension=0, tiled=True)
    total_b = lax.psum_scatter(
        part_b, "col", scatter_dimension=0, tiled=True, axis_index_groups=BACKWARD
    )

    activated, slopes = [], []
    for h, total in enumerate((total_a, total_b)):
        result, pullback = jax.vjp(gelu_tanh, total.astype(F32))
        activated.append(result.astype(BF16))
        cotangent = d_act[:, h * half : (h + 1) * half].astype(F32)
        slopes.append(pullback(cotangent)[0].astype(BF16))
    slopes_a = lax.all_gather(slopes[0], "col", axis=0, tiled=True)
    slopes_b = lax.all_gather(
        slopes[1], "col", axis=0, tiled=True, axis_index_groups=BACKWARD
    )

    slopes_all, own, other = partial_normed(slopes_a, slopes_b, weight, 256)
    d_weight = lax.dot_general(
        gathered, slopes_all, (((0,), (0,)), ((), ())), preferred_element_type=F32
    ).astype(BF16)

    chip_sum = (own.astype(F32) + send_core(other).astype(F32)).astype(BF16)
    arrived = lax.all_to_all(chip_sum.reshape(CHIPS, OWN, depth), ("x", "y"), 0, 0)
    d_normed = jnp.sum(arrived.astype(F32), axis=0).astype(BF16)
    return (jnp.concatenate(activated, axis=1), d_normed, d_weight)


def solution(mesh):
    split = Mesh(mesh.devices.reshape(NX, NY, NC, NZ), ("x", "y", "core", "col"))
    row = ("x", "y", "core")
    return jax.shard_map(
        per_device,
        mesh=split,
        in_specs=(P(row, "col"), P("col"), P("col"), P("col", row), P("col", row)),
        out_specs=(P("col", row), P(row, "col"), P("col", row)),
        check_vma=False,
    )
```

```python
import functools

import jax
import jax.numpy as jnp
from jax import lax
from jax.experimental import pallas as pl
from jax.experimental.pallas import tpu as pltpu
from jax.sharding import PartitionSpec as P

D = 12288
F32, BF16 = jnp.float32, jnp.bfloat16

NX, NY, NC, NZ = 4, 4, 2, 8
SHIFT = (0, 2, 3, 1)
FAR_FIRST = (4, 5, 3, 6, 2, 7, 1)
TOKENS_OWN = 16
TOKENS_Z = 64
TOKENS = 512
KERNEL_VMEM = 48 << 20


def row_pairs(dx, dy, dc):
    pairs = []
    for x in range(NX):
        for y in range(NY):
            for c in range(NC):
                source = (x * NY + y) * NC + c
                target = (((x + dx) % NX) * NY + (y + dy) % NY) * NC + (c + dc) % NC
                pairs.append((source, target))
    return pairs


def send_row(value, dx=0, dy=0, dc=0):
    return lax.ppermute(value, "row", row_pairs(dx, dy, dc))


def send_col(value, dz):
    return lax.ppermute(value, "col", [(z, (z + dz) % NZ) for z in range(NZ)])


def token_offset(core_shift, x_shift, y_shift):
    row, col = lax.axis_index("row"), lax.axis_index("col")
    x, y, c = row // (NY * NC), (row // NC) % NY, row % NC
    block = (((x + x_shift) % NX) * NY + (y + y_shift) % NY) * NC + (c + core_shift) % NC
    offset = (block * TOKENS_OWN - col * TOKENS_Z + TOKENS) % TOKENS
    return pl.multiple_of(offset, TOKENS_OWN)


def first_kernel(*refs):
    pieces, (w_ref, normed_ref), outs = refs[:8], refs[8:10], refs[10:]

    @pl.when(pl.program_id(0) == 0)
    def _():
        for core_shift in range(2):
            for iy in range(4):
                for ix in range(4):
                    offset = token_offset(core_shift, NX - SHIFT[ix], NY - SHIFT[iy])
                    normed_ref[pl.ds(offset, TOKENS_OWN), :] = pieces[core_shift * 4 + iy][
                        ix * TOKENS_OWN : (ix + 1) * TOKENS_OWN, :
                    ]

    product = jnp.dot(normed_ref[...], w_ref[...], preferred_element_type=F32)
    for k in range(NZ):
        outs[k][...] = product[k * TOKENS_Z : (k + 1) * TOKENS_Z, :].astype(outs[k].dtype)


def partial_pre(pieces, weight, tile):
    depth, width = weight.shape
    return pl.pallas_call(
        first_kernel,
        grid=(width // tile,),
        in_specs=[pl.BlockSpec(v.shape, lambda j: (0, 0)) for v in pieces]
        + [pl.BlockSpec((depth, tile), lambda j: (0, j))],
        out_specs=[pl.BlockSpec((TOKENS, depth), lambda j: (0, 0))]
        + [pl.BlockSpec((TOKENS_Z, tile), lambda j: (0, j))] * NZ,
        out_shape=[jax.ShapeDtypeStruct((TOKENS, depth), BF16)]
        + [jax.ShapeDtypeStruct((TOKENS_Z, width), BF16)] * NZ,
        compiler_params=pltpu.CompilerParams(vmem_limit_bytes=KERNEL_VMEM),
        cost_estimate=pl.CostEstimate(
            flops=2 * TOKENS * depth * width, bytes_accessed=depth * width * 2, transcendentals=0
        ),
    )(*pieces, weight)


def third_kernel(*refs):
    pieces, w_ref, slopes_ref, outs, acc = refs[:8], refs[8], refs[9], refs[10:18], refs[18]

    @pl.when(pl.program_id(0) == 0)
    def _():
        for k in range(NZ):
            slopes_ref[k * TOKENS_Z : (k + 1) * TOKENS_Z, :] = pieces[k][...]

    acc[...] = lax.dot_general(
        slopes_ref[...], w_ref[...], (((1,), (1,)), ((), ())), preferred_element_type=F32
    )
    for core_shift in range(2):
        for iy in range(4):
            for ix in range(4):
                offset = token_offset(core_shift, SHIFT[ix], SHIFT[iy])
                outs[core_shift * 4 + iy][ix * TOKENS_OWN : (ix + 1) * TOKENS_OWN, :] = acc[
                    pl.ds(offset, TOKENS_OWN), :
                ].astype(BF16)


def partial_normed(pieces, weight, tile):
    depth, width = weight.shape
    return pl.pallas_call(
        third_kernel,
        grid=(depth // tile,),
        in_specs=[pl.BlockSpec(v.shape, lambda j: (0, 0)) for v in pieces]
        + [pl.BlockSpec((tile, width), lambda j: (j, 0))],
        out_specs=[pl.BlockSpec((TOKENS, width), lambda j: (0, 0))]
        + [pl.BlockSpec((TOKENS_Z, tile), lambda j: (0, j))] * 8,
        out_shape=[jax.ShapeDtypeStruct((TOKENS, width), BF16)]
        + [jax.ShapeDtypeStruct((TOKENS_Z, depth), BF16)] * 8,
        scratch_shapes=[pltpu.VMEM((TOKENS, tile), F32)],
        compiler_params=pltpu.CompilerParams(vmem_limit_bytes=KERNEL_VMEM),
        cost_estimate=pl.CostEstimate(
            flops=2 * TOKENS * depth * width, bytes_accessed=depth * width * 2, transcendentals=0
        ),
    )(*pieces, weight)


def gelu_tanh(value):
    return jax.nn.gelu(value, approximate=True)


def add(*values):
    total = values[0].astype(F32)
    for value in values[1:]:
        total = total + value.astype(F32)
    return total


def normalize(inputs, gain, bias):
    local = inputs.shape[1]
    local_mean = jnp.sum(inputs, axis=1) / local
    centered = inputs - local_mean[:, None]
    local_square = jnp.sum(centered * centered, axis=1)
    stats = jnp.stack([local_mean, local_square])
    every = lax.all_to_all(jnp.broadcast_to(stats[None], (NZ,) + stats.shape), "col", 0, 0)
    mean = jnp.mean(every[:, 0, :], axis=0)
    offset = every[:, 0, :] - mean[None, :]
    spread = (jnp.sum(every[:, 1, :], axis=0) + local * jnp.sum(offset * offset, axis=0)) / D
    scale = lax.rsqrt(spread + 1e-05)
    moved = centered + (local_mean - mean)[:, None]
    return (moved * scale[:, None] * gain[None, :] + bias[None, :]).astype(BF16)


def per_device(inputs, gain, bias, weight, d_act):
    normed = normalize(inputs, gain, bias)

    along_x = jnp.concatenate([normed] + [send_row(normed, dx=s) for s in SHIFT[1:]])
    along_y = [along_x] + [send_row(along_x, dy=s) for s in SHIFT[1:]]
    other = [send_row(v, dc=1) for v in along_y]

    gathered, *parts = partial_pre(along_y + other, weight, 384)
    arrived = [send_col(parts[k], k) for k in FAR_FIRST]
    result, pullback = jax.vjp(gelu_tanh, add(parts[0], *arrived))
    activated = result.astype(BF16)
    slopes = pullback(d_act.astype(F32))[0].astype(BF16)
    blocks = {k: send_col(slopes, -k) for k in FAR_FIRST}
    pieces = [slopes] + [blocks[k] for k in range(1, NZ)]

    slopes_all, *parts = partial_normed(pieces, weight, 384)
    d_weight = lax.dot_general(
        gathered, slopes_all, (((0,), (0,)), ((), ())), preferred_element_type=F32
    ).astype(BF16)

    sums = [add(parts[i], send_row(parts[4 + i], dc=1)) for i in range(4)]
    arrived = [send_row(sums[i].astype(BF16), dy=SHIFT[i]) for i in range(1, 4)]
    column = add(sums[0], *arrived)
    blocks = [column[i * TOKENS_OWN : (i + 1) * TOKENS_OWN] for i in range(4)]
    arrived = [send_row(blocks[i].astype(BF16), dx=SHIFT[i]) for i in range(1, 4)]
    d_normed = add(blocks[0], *arrived).astype(BF16)
    return (activated, d_normed, d_weight)


def solution(mesh):
    return jax.shard_map(
        per_device,
        mesh=mesh,
        in_specs=(P("row", "col"), P("col"), P("col"), P("col", "row"), P("col", "row")),
        out_specs=(P("col", "row"), P("row", "col"), P("col", "row")),
        check_vma=False,
    )
```

```python
import jax
import jax.numpy as jnp
from jax import lax
from jax.experimental import pallas as pl
from jax.experimental.pallas import tpu as pltpu
from jax.sharding import PartitionSpec as P

D = 12288
F32, BF16 = jnp.float32, jnp.bfloat16

NX, NY, NC, NZ = 4, 4, 2, 8
GATHER_SHIFT = (0, 2, 3, 1)
SUM_SHIFT = (0, 1, 3, 2)
TOKENS_OWN = 16
TOKENS_Z = 64
TOKENS = 512
HALF = TOKENS // 2
KERNEL_VMEM = 48 << 20


def pairs_of(target):
    pairs = []
    for x in range(NX):
        for y in range(NY):
            for c in range(NC):
                for z in range(NZ):
                    source = ((x * NY + y) * NC + c) * NZ + z
                    tx, ty, tc, tz = target(x, y, c, z)
                    place = ((tx % NX) * NY + ty % NY) * NC + tc % NC
                    pairs.append((source, place * NZ + tz % NZ))
    return pairs


def send(value, target):
    return lax.ppermute(value, ("row", "col"), pairs_of(target))


def send_x(value, shift):
    return send(value, lambda x, y, c, z: (x + shift, y, c, z))


def send_y(value, shift):
    return send(value, lambda x, y, c, z: (x, y + shift, c, z))


def send_plane(value, shift, x_core):
    return send(
        value,
        lambda x, y, c, z: (x + shift, y, c, z) if c == x_core else (x, y + shift, c, z),
    )


def send_core(value):
    return send(value, lambda x, y, c, z: (x, y, c + 1, z))


def send_ring(value, way):
    return send(value, lambda x, y, c, z: (x, y, c, z + way * (1 - 2 * c)))


def row_of(block):
    row, col = lax.axis_index("row"), lax.axis_index("col")
    own = TOKENS_Z // TOKENS_OWN
    place = ((block // own - col) * (1 - 2 * (row % NC)) + 1 + 2 * NZ) % NZ
    return pl.multiple_of(place * TOKENS_Z + (block % own) * TOKENS_OWN, TOKENS_OWN)


def gathered_row(core_shift, i, p):
    row = lax.axis_index("row")
    x, y, c = row // (NY * NC), (row // NC) % NY, row % NC
    x, y = (x + NX - GATHER_SHIFT[p]) % NX, (y + NY - GATHER_SHIFT[i]) % NY
    return row_of((x * NY + y) * NC + (c + core_shift) % NC)


def summed_row(core_shift, i, p):
    row = lax.axis_index("row")
    x, y, c = row // (NY * NC), (row // NC) % NY, row % NC
    core = (c + core_shift) % NC
    x = (x + jnp.where(core == 1, SUM_SHIFT[i], SUM_SHIFT[p])) % NX
    y = (y + jnp.where(core == 1, SUM_SHIFT[p], SUM_SHIFT[i])) % NY
    return row_of((x * NY + y) * NC + core)


def store_blocks(product, outs):
    for k, out in enumerate(outs):
        out[...] = product[k * TOKENS_Z : (k + 1) * TOKENS_Z, :].astype(out.dtype)


def far_kernel(*refs):
    pieces, w_ref, normed_ref, outs = refs[:8], refs[8], refs[9], refs[10:]

    @pl.when(pl.program_id(0) == 0)
    def _():
        for core_shift in range(2):
            for i in range(4):
                for p in range(4):
                    rows = pl.ds(gathered_row(core_shift, i, p), TOKENS_OWN)
                    normed_ref[rows, :] = pieces[core_shift * 4 + i][
                        p * TOKENS_OWN : (p + 1) * TOKENS_OWN, :
                    ]

    store_blocks(
        jnp.dot(normed_ref[HALF:, :], w_ref[...], preferred_element_type=F32), outs
    )


def near_kernel(normed_ref, w_ref, *outs):
    store_blocks(jnp.dot(normed_ref[...], w_ref[...], preferred_element_type=F32), outs)


def whole(shape):
    return pl.BlockSpec(shape, lambda j: (0, 0))


def settings(depth, width):
    return dict(
        compiler_params=pltpu.CompilerParams(vmem_limit_bytes=KERNEL_VMEM),
        cost_estimate=pl.CostEstimate(
            flops=TOKENS * depth * width, bytes_accessed=depth * width * 2, transcendentals=0
        ),
    )


def far_pre(pieces, weight, tile):
    depth, width = weight.shape
    return pl.pallas_call(
        far_kernel,
        grid=(width // tile,),
        in_specs=[whole(v.shape) for v in pieces] + [pl.BlockSpec((depth, tile), lambda j: (0, j))],
        out_specs=[whole((TOKENS, depth))]
        + [pl.BlockSpec((TOKENS_Z, tile), lambda j: (0, j))] * (NZ // 2),
        out_shape=[jax.ShapeDtypeStruct((TOKENS, depth), BF16)]
        + [jax.ShapeDtypeStruct((TOKENS_Z, width), BF16)] * (NZ // 2),
        **settings(depth, width),
    )(*pieces, weight)


def near_pre(normed, weight, tile):
    depth, width = weight.shape
    return pl.pallas_call(
        near_kernel,
        grid=(width // tile,),
        in_specs=[whole((HALF, depth)), pl.BlockSpec((depth, tile), lambda j: (0, j))],
        out_specs=[pl.BlockSpec((TOKENS_Z, tile), lambda j: (0, j))] * (NZ // 2),
        out_shape=[jax.ShapeDtypeStruct((TOKENS_Z, width), BF16)] * (NZ // 2),
        **settings(depth, width),
    )(normed, weight)


def transposed_dot(rows, weight):
    return lax.dot_general(rows, weight, (((1,), (1,)), ((), ())), preferred_element_type=F32)


def near_back_kernel(*refs):
    pieces, w_ref, out_ref, rows = refs[:4], refs[4], refs[5], refs[6]

    @pl.when(pl.program_id(0) == 0)
    def _():
        for k in range(4):
            rows[k * TOKENS_Z : (k + 1) * TOKENS_Z, :] = pieces[k][...]

    out_ref[...] = transposed_dot(rows[...], w_ref[...]).astype(out_ref.dtype)


def near_back(pieces, weight, tile):
    depth, width = weight.shape
    return pl.pallas_call(
        near_back_kernel,
        grid=(depth // tile,),
        in_specs=[whole(v.shape) for v in pieces] + [pl.BlockSpec((tile, width), lambda j: (j, 0))],
        out_specs=pl.BlockSpec((HALF, tile), lambda j: (0, j)),
        out_shape=jax.ShapeDtypeStruct((HALF, depth), BF16),
        scratch_shapes=[pltpu.VMEM((HALF, width), BF16)],
        **settings(depth, width),
    )(*pieces, weight)


def far_back_kernel(*refs):
    pieces, near_ref, w_ref, slopes_ref, outs, product = (
        refs[:8], refs[8], refs[9], refs[10], refs[11:19], refs[19]
    )

    @pl.when(pl.program_id(0) == 0)
    def _():
        for k in range(NZ):
            slopes_ref[k * TOKENS_Z : (k + 1) * TOKENS_Z, :] = pieces[k][...]

    product[:HALF, :] = near_ref[...].astype(F32)
    product[HALF:, :] = transposed_dot(slopes_ref[HALF:, :], w_ref[...])
    for core_shift in range(2):
        for i in range(4):
            for p in range(4):
                outs[core_shift * 4 + i][p * TOKENS_OWN : (p + 1) * TOKENS_OWN, :] = product[
                    pl.ds(summed_row(core_shift, i, p), TOKENS_OWN), :
                ].astype(BF16)


def far_back(pieces, near, weight, tile):
    depth, width = weight.shape
    return pl.pallas_call(
        far_back_kernel,
        grid=(depth // tile,),
        in_specs=[whole(v.shape) for v in pieces]
        + [pl.BlockSpec((HALF, tile), lambda j: (0, j))]
        + [pl.BlockSpec((tile, width), lambda j: (j, 0))],
        out_specs=[whole((TOKENS, width))] + [pl.BlockSpec((TOKENS_Z, tile), lambda j: (0, j))] * 8,
        out_shape=[jax.ShapeDtypeStruct((TOKENS, width), BF16)]
        + [jax.ShapeDtypeStruct((TOKENS_Z, depth), BF16)] * 8,
        scratch_shapes=[pltpu.VMEM((TOKENS, tile), F32)],
        **settings(depth, width),
    )(*pieces, near, weight)


def gelu_tanh(value):
    return jax.nn.gelu(value, approximate=True)


def add(*values):
    total = values[0].astype(F32)
    for value in values[1:]:
        total = total + value.astype(F32)
    return total


def normalize(inputs, gain, bias):
    local = inputs.shape[1]
    local_mean = jnp.sum(inputs, axis=1) / local
    centered = inputs - local_mean[:, None]
    local_square = jnp.sum(centered * centered, axis=1)
    stats = jnp.stack([local_mean, local_square])
    every = lax.all_to_all(jnp.broadcast_to(stats[None], (NZ,) + stats.shape), "col", 0, 0)
    mean = jnp.mean(every[:, 0, :], axis=0)
    offset = every[:, 0, :] - mean[None, :]
    spread = (jnp.sum(every[:, 1, :], axis=0) + local * jnp.sum(offset * offset, axis=0)) / D
    scale = lax.rsqrt(spread + 1e-05)
    moved = centered + (local_mean - mean)[:, None]
    return (moved * scale[:, None] * gain[None, :] + bias[None, :]).astype(BF16)


def reduce_chain(parts, way):
    travelling = send_ring(parts[0], way)
    for part in parts[1:]:
        travelling = send_ring(add(part, travelling).astype(BF16), way)
    return travelling


def gather_chain(own, way, count):
    got = []
    for _ in range(count):
        own = send_ring(own, way)
        got.append(own)
    return got


def per_device(inputs, gain, bias, weight, d_act):
    normed = normalize(inputs, gain, bias)

    along_x = jnp.concatenate([normed] + [send_x(normed, s) for s in GATHER_SHIFT[1:]])
    along_y = [along_x] + [send_y(along_x, s) for s in GATHER_SHIFT[1:]]
    other = [send_core(v) for v in along_y]

    gathered, *far = far_pre(along_y + other, weight, 512)
    back, own, one, two = near_pre(gathered, weight, 512)
    forward = reduce_chain([far[1], far[0], two, one], 1)
    backward = reduce_chain([far[2], far[3], back], -1)

    result, pullback = jax.vjp(gelu_tanh, add(own, forward, backward))
    activated = result.astype(BF16)
    slopes = pullback(d_act.astype(F32))[0].astype(BF16)
    behind = gather_chain(slopes, 1, 4)
    ahead = gather_chain(slopes, -1, 3)
    pieces = [behind[0], slopes] + ahead + behind[:0:-1]

    near = near_back(pieces[:4], weight, 512)
    slopes_all, *parts = far_back(pieces, near, weight, 512)
    d_weight = lax.dot_general(
        gathered, slopes_all, (((0,), (0,)), ((), ())), preferred_element_type=F32
    ).astype(BF16)

    sums = [add(parts[i], send_core(parts[4 + i])) for i in range(4)]
    arrived = [send_plane(sums[i].astype(BF16), SUM_SHIFT[i], 1) for i in range(1, 4)]
    line = add(sums[0], *arrived)
    line, d_weight = lax.optimization_barrier((line, d_weight))
    blocks = [line[i * TOKENS_OWN : (i + 1) * TOKENS_OWN] for i in range(4)]
    arrived = [send_plane(blocks[i].astype(BF16), SUM_SHIFT[i], 0) for i in range(1, 4)]
    d_normed = add(blocks[0], *arrived).astype(BF16)
    return (activated, d_normed, d_weight)


def solution(mesh):
    return jax.shard_map(
        per_device,
        mesh=mesh,
        in_specs=(P("row", "col"), P("col"), P("col"), P("col", "row"), P("col", "row")),
        out_specs=(P("col", "row"), P("row", "col"), P("col", "row")),
        check_vma=False,
    )
```

```python
import jax
import jax.numpy as jnp
from jax import lax
from jax.experimental import pallas as pl
from jax.experimental.pallas import tpu as pltpu
from jax.sharding import PartitionSpec as P

D = 12288
F32, BF16 = jnp.float32, jnp.bfloat16

NX, NY, NC, NZ = 4, 4, 2, 8
GATHER_SHIFT = (0, 2, 3, 1)
SUM_SHIFT = (0, 1, 3, 2)
TOKENS_OWN = 16
TOKENS_Z = 64
TOKENS = 512
HALF = TOKENS // 2


def pairs_of(target):
    pairs = []
    for x in range(NX):
        for y in range(NY):
            for c in range(NC):
                for z in range(NZ):
                    source = ((x * NY + y) * NC + c) * NZ + z
                    tx, ty, tc, tz = target(x, y, c, z)
                    place = ((tx % NX) * NY + ty % NY) * NC + tc % NC
                    pairs.append((source, place * NZ + tz % NZ))
    return pairs


def send(value, target):
    return lax.ppermute(value, ("row", "col"), pairs_of(target))


def send_x(value, shift):
    return send(value, lambda x, y, c, z: (x + shift, y, c, z))


def send_y(value, shift):
    return send(value, lambda x, y, c, z: (x, y + shift, c, z))


def send_plane(value, shift, x_core):
    return send(
        value,
        lambda x, y, c, z: (x + shift, y, c, z) if c == x_core else (x, y + shift, c, z),
    )


def send_core(value):
    return send(value, lambda x, y, c, z: (x, y, c + 1, z))


def send_ring(value, way):
    return send(value, lambda x, y, c, z: (x, y, c, z + way * (1 - 2 * ((z + c) % 2))))


def row_of(block):
    row, col = lax.axis_index("row"), lax.axis_index("col")
    own = TOKENS_Z // TOKENS_OWN
    place = ((block // own - col) * (1 - 2 * ((row + col) % 2)) + 1 + 2 * NZ) % NZ
    return pl.multiple_of(place * TOKENS_Z + (block % own) * TOKENS_OWN, TOKENS_OWN)


def gathered_row(core_shift, i, p):
    row = lax.axis_index("row")
    x, y, c = row // (NY * NC), (row // NC) % NY, row % NC
    x, y = (x + NX - GATHER_SHIFT[p]) % NX, (y + NY - GATHER_SHIFT[i]) % NY
    return row_of((x * NY + y) * NC + (c + core_shift) % NC)


def summed_row(core_shift, i, p):
    row = lax.axis_index("row")
    x, y, c = row // (NY * NC), (row // NC) % NY, row % NC
    core = (c + core_shift) % NC
    x = (x + jnp.where(core == 1, SUM_SHIFT[i], SUM_SHIFT[p])) % NX
    y = (y + jnp.where(core == 1, SUM_SHIFT[p], SUM_SHIFT[i])) % NY
    return row_of((x * NY + y) * NC + core)


WHOLE = pl.BlockSpec(memory_space=pltpu.VMEM)
TILE = 512


def settings(weight, limit):
    depth, width = weight.shape
    return dict(
        compiler_params=pltpu.CompilerParams(vmem_limit_bytes=limit << 20),
        cost_estimate=pl.CostEstimate(
            flops=TOKENS * depth * width, bytes_accessed=depth * width * 2, transcendentals=0
        ),
    )


def stage_kernel(w_ref, out_ref, sem):
    copy = pltpu.make_async_copy(w_ref, out_ref, sem)
    copy.start()
    copy.wait()


def stage(weight):
    return pl.pallas_call(
        stage_kernel,
        in_specs=[pl.BlockSpec(memory_space=pl.ANY)],
        out_specs=WHOLE,
        out_shape=jax.ShapeDtypeStruct(weight.shape, weight.dtype),
        scratch_shapes=[pltpu.SemaphoreType.DMA],
        **settings(weight, 48),
    )(weight)


def multiply(rows, w_ref, outs):
    for start in range(0, w_ref.shape[1], TILE):
        columns = slice(start, start + TILE)
        product = jnp.dot(rows, w_ref[:, columns], preferred_element_type=F32)
        for k, out in enumerate(outs):
            out[:, columns] = product[k * TOKENS_Z : (k + 1) * TOKENS_Z, :].astype(out.dtype)


def far_kernel(*refs):
    pieces, w_ref, normed_ref, outs = refs[:8], refs[8], refs[9], refs[10:]
    for core_shift in range(2):
        for i in range(4):
            for p in range(4):
                rows = pl.ds(gathered_row(core_shift, i, p), TOKENS_OWN)
                normed_ref[rows, :] = pieces[core_shift * 4 + i][
                    p * TOKENS_OWN : (p + 1) * TOKENS_OWN, :
                ]
    multiply(normed_ref[HALF:, :], w_ref, outs)


def near_kernel(normed_ref, w_ref, *outs):
    multiply(normed_ref[:HALF, :], w_ref, outs)


def far_pre(pieces, weight):
    depth, width = weight.shape
    return pl.pallas_call(
        far_kernel,
        in_specs=[WHOLE] * 9,
        out_specs=[WHOLE] * 5,
        out_shape=[jax.ShapeDtypeStruct((TOKENS, depth), BF16)]
        + [jax.ShapeDtypeStruct((TOKENS_Z, width), BF16)] * 4,
        **settings(weight, 16),
    )(*pieces, weight)


def near_pre(normed, weight):
    return pl.pallas_call(
        near_kernel,
        in_specs=[WHOLE] * 2,
        out_specs=[WHOLE] * 4,
        out_shape=[jax.ShapeDtypeStruct((TOKENS_Z, weight.shape[1]), BF16)] * 4,
        **settings(weight, 16),
    )(normed, weight)


def transposed_dot(rows, weight):
    return lax.dot_general(rows, weight, (((1,), (1,)), ((), ())), preferred_element_type=F32)


def near_back_kernel(*refs):
    pieces, w_ref, out_ref = refs[:4], refs[4], refs[5]
    rows = jnp.concatenate([piece[...] for piece in pieces], axis=0)
    for start in range(0, w_ref.shape[0], TILE):
        part = slice(start, start + TILE)
        out_ref[:, part] = transposed_dot(rows, w_ref[part, :]).astype(out_ref.dtype)


def near_back(pieces, weight):
    return pl.pallas_call(
        near_back_kernel,
        in_specs=[WHOLE] * 5,
        out_specs=WHOLE,
        out_shape=jax.ShapeDtypeStruct((HALF, weight.shape[0]), BF16),
        **settings(weight, 16),
    )(*pieces, weight)


def far_back_kernel(*refs):
    pieces, near_ref, w_ref, slopes_ref, outs, product = (
        refs[:8], refs[8], refs[9], refs[10], refs[11:19], refs[19]
    )
    for k in range(NZ):
        slopes_ref[k * TOKENS_Z : (k + 1) * TOKENS_Z, :] = pieces[k][...]
    product[:HALF, :] = near_ref[...].astype(F32)
    rows = slopes_ref[HALF:, :]
    for start in range(0, w_ref.shape[0], TILE):
        part = slice(start, start + TILE)
        product[HALF:, part] = transposed_dot(rows, w_ref[part, :])
    for core_shift in (1, 0):
        for i in range(4):
            for p in range(4):
                outs[core_shift * 4 + i][p * TOKENS_OWN : (p + 1) * TOKENS_OWN, :] = product[
                    pl.ds(summed_row(core_shift, i, p), TOKENS_OWN), :
                ].astype(BF16)


def far_back(pieces, near, weight):
    depth, width = weight.shape
    return pl.pallas_call(
        far_back_kernel,
        in_specs=[WHOLE] * 10,
        out_specs=[WHOLE] * 9,
        out_shape=[jax.ShapeDtypeStruct((TOKENS, width), BF16)]
        + [jax.ShapeDtypeStruct((TOKENS_Z, depth), BF16)] * 8,
        scratch_shapes=[pltpu.VMEM((TOKENS, depth), F32)],
        **settings(weight, 16),
    )(*pieces, near, weight)


def gelu_tanh(value):
    return jax.nn.gelu(value, approximate=True)


def add(*values):
    total = values[0].astype(F32)
    for value in values[1:]:
        total = total + value.astype(F32)
    return total


def normalize(inputs, gain, bias):
    local = inputs.shape[1]
    local_mean = jnp.sum(inputs, axis=1) / local
    centered = inputs - local_mean[:, None]
    local_square = jnp.sum(centered * centered, axis=1)
    stats = jnp.stack([local_mean, local_square])
    every = lax.all_to_all(jnp.broadcast_to(stats[None], (NZ,) + stats.shape), "col", 0, 0)
    mean = jnp.mean(every[:, 0, :], axis=0)
    offset = every[:, 0, :] - mean[None, :]
    spread = (jnp.sum(every[:, 1, :], axis=0) + local * jnp.sum(offset * offset, axis=0)) / D
    scale = lax.rsqrt(spread + 1e-05)
    moved = centered + (local_mean - mean)[:, None]
    return (moved * scale[:, None] * gain[None, :] + bias[None, :]).astype(BF16)


def reduce_chain(parts):
    travelling = send_ring(parts[0], 1)
    for step, part in enumerate(parts[1:]):
        travelling = send_ring(add(part, travelling).astype(BF16), 2 * (step % 2) - 1)
    return travelling


def gather_chain(own, way, count):
    got = []
    for _ in range(count):
        own = send_ring(own, way)
        way = -way
        got.append(own)
    return got


def per_device(inputs, gain, bias, weight, d_act):
    normed = normalize(inputs, gain, bias)

    along_x = jnp.concatenate([normed] + [send_x(normed, s) for s in GATHER_SHIFT[1:]])
    along_y = [along_x] + [send_y(along_x, s) for s in GATHER_SHIFT[1:]]
    weight, _ = lax.optimization_barrier((weight, along_x))
    along_y[3], weight = lax.optimization_barrier((along_y[3], stage(weight)))
    other = [send_core(v) for v in along_y]

    gathered, *far = far_pre(along_y + other, weight)
    back, own, one, two = near_pre(gathered, weight)
    longer = reduce_chain([far[1], far[2], two, back])
    shorter = reduce_chain([far[0], far[3], one])

    pre = add(own, longer, shorter)
    slopes = jax.vjp(gelu_tanh, pre)[1](d_act.astype(F32))[0].astype(BF16)
    block_1, block_6, block_3, block_4 = gather_chain(slopes, 1, 4)
    block_7, block_2, block_5 = gather_chain(slopes, -1, 3)
    pieces = [block_7, slopes, block_1, block_2, block_3, block_4, block_5, block_6]
    pre, _ = lax.optimization_barrier((pre, block_1))
    activated = gelu_tanh(pre).astype(BF16)

    near = near_back(pieces[:4], weight)
    slopes_all, *parts = far_back(pieces, near, weight)
    d_weight = lax.dot_general(
        gathered, slopes_all, (((0,), (0,)), ((), ())), preferred_element_type=F32
    ).astype(BF16)

    sums = [add(parts[i], send_core(parts[4 + i])) for i in range(4)]
    arrived = [send_plane(sums[i].astype(BF16), SUM_SHIFT[i], 1) for i in range(1, 4)]
    line = add(sums[0], *arrived)
    line, d_weight = lax.optimization_barrier((line, d_weight))
    blocks = [line[i * TOKENS_OWN : (i + 1) * TOKENS_OWN] for i in range(4)]
    arrived = [send_plane(blocks[i].astype(BF16), SUM_SHIFT[i], 0) for i in range(1, 4)]
    d_normed = add(blocks[0], *arrived).astype(BF16)
    return (activated, d_normed, d_weight)


def solution(mesh):
    return jax.shard_map(
        per_device,
        mesh=mesh,
        in_specs=(P("row", "col"), P("col"), P("col"), P("col", "row"), P("col", "row")),
        out_specs=(P("col", "row"), P("row", "col"), P("col", "row")),
        check_vma=False,
    )
```

```python
import jax
import jax.numpy as jnp
from jax import lax
from jax.experimental import pallas as pl
from jax.experimental.pallas import tpu as pltpu
from jax.sharding import PartitionSpec as P

D = 12288
F32, BF16 = jnp.float32, jnp.bfloat16

NX, NY, NC, NZ = 4, 4, 2, 8
GATHER_SHIFT = (0, 2, 3, 1)
SUM_SHIFT = (0, 1, 3, 2)
TOKENS_OWN = 16
TOKENS_Z = 64
TOKENS = 512
HALF = TOKENS // 2


def pairs_of(target):
    pairs = []
    for x in range(NX):
        for y in range(NY):
            for c in range(NC):
                for z in range(NZ):
                    source = ((x * NY + y) * NC + c) * NZ + z
                    tx, ty, tc, tz = target(x, y, c, z)
                    place = ((tx % NX) * NY + ty % NY) * NC + tc % NC
                    pairs.append((source, place * NZ + tz % NZ))
    return pairs


def send(value, target):
    return lax.ppermute(value, ("row", "col"), pairs_of(target))


def send_x(value, shift):
    return send(value, lambda x, y, c, z: (x + shift, y, c, z))


def send_y(value, shift):
    return send(value, lambda x, y, c, z: (x, y + shift, c, z))


def send_plane(value, shift, x_core):
    return send(
        value,
        lambda x, y, c, z: (x + shift, y, c, z) if c == x_core else (x, y + shift, c, z),
    )


def send_core(value):
    return send(value, lambda x, y, c, z: (x, y, c + 1, z))


def send_ring(value, way, hops=1):
    return send(value, lambda x, y, c, z: (x, y, c, z + way * hops * (1 - 2 * ((z + c) % 2))))


def row_of(block):
    row, col = lax.axis_index("row"), lax.axis_index("col")
    own = TOKENS_Z // TOKENS_OWN
    place = ((block // own - col) * (1 - 2 * ((row + col) % 2)) + 1 + 2 * NZ) % NZ
    return pl.multiple_of(place * TOKENS_Z + (block % own) * TOKENS_OWN, TOKENS_OWN)


def gathered_row(core_shift, i, p):
    row = lax.axis_index("row")
    x, y, c = row // (NY * NC), (row // NC) % NY, row % NC
    x, y = (x + NX - GATHER_SHIFT[p]) % NX, (y + NY - GATHER_SHIFT[i]) % NY
    return row_of((x * NY + y) * NC + (c + core_shift) % NC)


def summed_row(core_shift, i, p):
    row = lax.axis_index("row")
    x, y, c = row // (NY * NC), (row // NC) % NY, row % NC
    core = (c + core_shift) % NC
    x = (x + jnp.where(core == 1, SUM_SHIFT[i], SUM_SHIFT[p])) % NX
    y = (y + jnp.where(core == 1, SUM_SHIFT[p], SUM_SHIFT[i])) % NY
    return row_of((x * NY + y) * NC + core)


WHOLE = pl.BlockSpec(memory_space=pltpu.VMEM)
TILE = 512


def settings(weight, limit):
    depth, width = weight.shape
    return dict(
        compiler_params=pltpu.CompilerParams(vmem_limit_bytes=limit << 20),
        cost_estimate=pl.CostEstimate(
            flops=TOKENS * depth * width, bytes_accessed=depth * width * 2, transcendentals=0
        ),
    )


def stage_kernel(w_ref, out_ref, sem):
    copy = pltpu.make_async_copy(w_ref, out_ref, sem)
    copy.start()
    copy.wait()


def stage(weight):
    return pl.pallas_call(
        stage_kernel,
        in_specs=[pl.BlockSpec(memory_space=pl.ANY)],
        out_specs=WHOLE,
        out_shape=jax.ShapeDtypeStruct(weight.shape, weight.dtype),
        scratch_shapes=[pltpu.SemaphoreType.DMA],
        **settings(weight, 48),
    )(weight)


def multiply(rows, w_ref, outs):
    for start in range(0, w_ref.shape[1], TILE):
        columns = slice(start, start + TILE)
        product = jnp.dot(rows, w_ref[:, columns], preferred_element_type=F32)
        for k, out in enumerate(outs):
            out[:, columns] = product[k * TOKENS_Z : (k + 1) * TOKENS_Z, :].astype(out.dtype)


def far_kernel(*refs):
    pieces, w_ref, normed_ref, outs = refs[:8], refs[8], refs[9], refs[10:]
    for core_shift in range(2):
        for i in range(4):
            for p in range(4):
                rows = pl.ds(gathered_row(core_shift, i, p), TOKENS_OWN)
                normed_ref[rows, :] = pieces[core_shift * 4 + i][
                    p * TOKENS_OWN : (p + 1) * TOKENS_OWN, :
                ]
    multiply(normed_ref[HALF:, :], w_ref, outs)


def near_kernel(normed_ref, w_ref, *outs):
    multiply(normed_ref[:HALF, :], w_ref, outs)


def far_pre(pieces, weight):
    depth, width = weight.shape
    return pl.pallas_call(
        far_kernel,
        in_specs=[WHOLE] * 9,
        out_specs=[WHOLE] * 5,
        out_shape=[jax.ShapeDtypeStruct((TOKENS, depth), BF16)]
        + [jax.ShapeDtypeStruct((TOKENS_Z, width), BF16)] * 4,
        **settings(weight, 16),
    )(*pieces, weight)


def near_pre(normed, weight):
    return pl.pallas_call(
        near_kernel,
        in_specs=[WHOLE] * 2,
        out_specs=[WHOLE] * 4,
        out_shape=[jax.ShapeDtypeStruct((TOKENS_Z, weight.shape[1]), BF16)] * 4,
        **settings(weight, 16),
    )(normed, weight)


def transposed_dot(rows, weight):
    return lax.dot_general(rows, weight, (((1,), (1,)), ((), ())), preferred_element_type=F32)


def near_back_kernel(*refs):
    pieces, w_ref, out_ref = refs[:4], refs[4], refs[5]
    rows = jnp.concatenate([piece[...] for piece in pieces], axis=0)
    for start in range(0, w_ref.shape[0], TILE):
        part = slice(start, start + TILE)
        out_ref[:, part] = transposed_dot(rows, w_ref[part, :]).astype(out_ref.dtype)


def near_back(pieces, weight):
    return pl.pallas_call(
        near_back_kernel,
        in_specs=[WHOLE] * 5,
        out_specs=WHOLE,
        out_shape=jax.ShapeDtypeStruct((HALF, weight.shape[0]), BF16),
        **settings(weight, 16),
    )(*pieces, weight)


def far_back_kernel(*refs):
    pieces, near_ref, w_ref, slopes_ref, outs, product = (
        refs[:8], refs[8], refs[9], refs[10], refs[11:19], refs[19]
    )
    for k in range(NZ):
        slopes_ref[k * TOKENS_Z : (k + 1) * TOKENS_Z, :] = pieces[k][...]
    product[:HALF, :] = near_ref[...].astype(F32)
    rows = slopes_ref[HALF:, :]
    for start in range(0, w_ref.shape[0], TILE):
        part = slice(start, start + TILE)
        product[HALF:, part] = transposed_dot(rows, w_ref[part, :])
    for core_shift in (1, 0):
        for i in range(4):
            for p in range(4):
                outs[core_shift * 4 + i][p * TOKENS_OWN : (p + 1) * TOKENS_OWN, :] = product[
                    pl.ds(summed_row(core_shift, i, p), TOKENS_OWN), :
                ].astype(BF16)


def far_back(pieces, near, weight):
    depth, width = weight.shape
    return pl.pallas_call(
        far_back_kernel,
        in_specs=[WHOLE] * 10,
        out_specs=[WHOLE] * 9,
        out_shape=[jax.ShapeDtypeStruct((TOKENS, width), BF16)]
        + [jax.ShapeDtypeStruct((TOKENS_Z, depth), BF16)] * 8,
        scratch_shapes=[pltpu.VMEM((TOKENS, depth), F32)],
        **settings(weight, 16),
    )(*pieces, near, weight)


def gelu_tanh(value):
    return jax.nn.gelu(value, approximate=True)


def add(*values):
    total = values[0].astype(F32)
    for value in values[1:]:
        total = total + value.astype(F32)
    return total


def center_kernel(inputs_ref, centered_ref, mean_ref, square_ref):
    rows = inputs_ref[...]
    mean = jnp.sum(rows, axis=1, keepdims=True) / rows.shape[1]
    centered = rows - mean
    centered_ref[...] = centered
    mean_ref[...] = mean
    square_ref[...] = jnp.sum(centered * centered, axis=1, keepdims=True)


def center(inputs):
    column = jax.ShapeDtypeStruct((inputs.shape[0], 1), F32)
    return pl.pallas_call(
        center_kernel,
        in_specs=[WHOLE],
        out_specs=[WHOLE] * 3,
        out_shape=[jax.ShapeDtypeStruct(inputs.shape, F32), column, column],
    )(inputs)


def normalize(inputs, gain, bias):
    local = inputs.shape[1]
    centered, local_mean, local_square = center(inputs)
    local_mean = local_mean[:, 0]
    stats = jnp.stack([local_mean, local_square[:, 0]])
    every = lax.all_to_all(jnp.broadcast_to(stats[None], (NZ,) + stats.shape), "col", 0, 0)
    mean = jnp.mean(every[:, 0, :], axis=0)
    offset = every[:, 0, :] - mean[None, :]
    spread = (jnp.sum(every[:, 1, :], axis=0) + local * jnp.sum(offset * offset, axis=0)) / D
    scale = lax.rsqrt(spread + 1e-05)
    moved = centered + (local_mean - mean)[:, None]
    return (moved * scale[:, None] * gain[None, :] + bias[None, :]).astype(BF16)


def per_device(inputs, gain, bias, weight, d_act):
    normed = normalize(inputs, gain, bias)

    along_x = jnp.concatenate([normed] + [send_x(normed, s) for s in GATHER_SHIFT[1:]])
    along_y = [along_x] + [send_y(along_x, s) for s in GATHER_SHIFT[1:]]
    weight, _ = lax.optimization_barrier((weight, along_x))
    along_y[3], weight = lax.optimization_barrier((along_y[3], stage(weight)))
    other = [send_core(v) for v in along_y]

    gathered, *far = far_pre(along_y + other, weight)
    back, own, one, two = near_pre(gathered, weight)
    four = send_ring(far[1], 1, 2)
    three = send_ring(far[0], 1)
    five = send_ring(far[2], -1)
    two = send_ring(add(two, four, five).astype(BF16), 1)
    six = send_ring(add(far[3], three).astype(BF16), -1)
    back = send_ring(add(back, two).astype(BF16), -1)
    one = send_ring(add(one, six).astype(BF16), 1)

    pre = add(own, back, one)
    slopes = jax.vjp(gelu_tanh, pre)[1](d_act.astype(F32))[0].astype(BF16)
    block_1 = send_ring(slopes, 1)
    block_7 = send_ring(slopes, -1)
    block_6 = send_ring(block_1, -1)
    block_2 = send_ring(block_7, 1)
    block_4 = send_ring(block_2, -1, 2)
    block_3 = send_ring(block_6, 1)
    block_5 = send_ring(block_2, -1)
    pieces = [block_7, slopes, block_1, block_2, block_3, block_4, block_5, block_6]
    pre, _ = lax.optimization_barrier((pre, block_1))
    activated = gelu_tanh(pre).astype(BF16)

    near = near_back(pieces[:4], weight)
    slopes_all, *parts = far_back(pieces, near, weight)
    d_weight = lax.dot_general(
        gathered, slopes_all, (((0,), (0,)), ((), ())), preferred_element_type=F32
    ).astype(BF16)

    sums = [add(parts[i], send_core(parts[4 + i])) for i in range(4)]
    arrived = [send_plane(sums[i].astype(BF16), SUM_SHIFT[i], 1) for i in range(1, 4)]
    line = add(sums[0], *arrived)
    line, d_weight = lax.optimization_barrier((line, d_weight))
    blocks = [line[i * TOKENS_OWN : (i + 1) * TOKENS_OWN] for i in range(4)]
    arrived = [send_plane(blocks[i].astype(BF16), SUM_SHIFT[i], 0) for i in range(1, 4)]
    d_normed = add(blocks[0], *arrived).astype(BF16)
    return (activated, d_normed, d_weight)


def solution(mesh):
    return jax.shard_map(
        per_device,
        mesh=mesh,
        in_specs=(P("row", "col"), P("col"), P("col"), P("col", "row"), P("col", "row")),
        out_specs=(P("col", "row"), P("row", "col"), P("col", "row")),
        check_vma=False,
    )
```

```python
import jax
import jax.numpy as jnp
from jax import lax
from jax.experimental import pallas as pl
from jax.experimental.pallas import tpu as pltpu
from jax.sharding import PartitionSpec as P

D = 12288
F32, BF16 = jnp.float32, jnp.bfloat16

NX, NY, NC, NZ = 4, 4, 2, 8
GATHER_X, GATHER_Y, SUM = (0, 1, 3, 2), (0, 2, 3, 1), (0, 1, 3, 2)
TOKENS_OWN = 16
TOKENS_Z = 64
TOKENS = 512
HALF = TOKENS // 2


def pairs_of(target):
    pairs = []
    for x in range(NX):
        for y in range(NY):
            for c in range(NC):
                for z in range(NZ):
                    source = ((x * NY + y) * NC + c) * NZ + z
                    tx, ty, tc, tz = target(x, y, c, z)
                    place = ((tx % NX) * NY + ty % NY) * NC + tc % NC
                    pairs.append((source, place * NZ + tz % NZ))
    return pairs


def send(value, target):
    return lax.ppermute(value, ("row", "col"), pairs_of(target))


def send_x(value, k):
    return send(value, lambda x, y, c, z: (x ^ k, y, c, z))


def send_y(value, k):
    return send(value, lambda x, y, c, z: (x, y ^ k, c, z))


def send_plane(value, k, x_core):
    return send(value, lambda x, y, c, z: (x ^ k, y, c, z) if c == x_core else (x, y ^ k, c, z))


def send_core(value):
    return send(value, lambda x, y, c, z: (x, y, c + 1, z))


def send_ring(value, way):
    return send(value, lambda x, y, c, z: (x, y, c, z + way * (1 - 2 * ((z + c) % 2))))


def row_of(block):
    row, col = lax.axis_index("row"), lax.axis_index("col")
    own = TOKENS_Z // TOKENS_OWN
    place = ((block // own - col) * (1 - 2 * ((row + col) % 2)) + 1 + 2 * NZ) % NZ
    return pl.multiple_of(place * TOKENS_Z + (block % own) * TOKENS_OWN, TOKENS_OWN)


def gathered_row(core_shift, i, p):
    row = lax.axis_index("row")
    x, y, c = row // (NY * NC), (row // NC) % NY, row % NC
    x, y = x ^ GATHER_X[p], y ^ GATHER_Y[i]
    return row_of((x * NY + y) * NC + (c + core_shift) % NC)


def summed_row(core_shift, i, p):
    row = lax.axis_index("row")
    x, y, c = row // (NY * NC), (row // NC) % NY, row % NC
    core = (c + core_shift) % NC
    x = x ^ jnp.where(core == 1, SUM[i], SUM[p])
    y = y ^ jnp.where(core == 1, SUM[p], SUM[i])
    return row_of((x * NY + y) * NC + core)


WHOLE = pl.BlockSpec(memory_space=pltpu.VMEM)
TILE = 512


def settings(weight, limit):
    depth, width = weight.shape
    return dict(
        compiler_params=pltpu.CompilerParams(vmem_limit_bytes=limit << 20),
        cost_estimate=pl.CostEstimate(
            flops=TOKENS * depth * width, bytes_accessed=depth * width * 2, transcendentals=0
        ),
    )


def stage_kernel(w_ref, out_ref, sem):
    copy = pltpu.make_async_copy(w_ref, out_ref, sem)
    copy.start()
    copy.wait()


def stage(weight):
    return pl.pallas_call(
        stage_kernel,
        in_specs=[pl.BlockSpec(memory_space=pl.ANY)],
        out_specs=WHOLE,
        out_shape=jax.ShapeDtypeStruct(weight.shape, weight.dtype),
        scratch_shapes=[pltpu.SemaphoreType.DMA],
        **settings(weight, 48),
    )(weight)


def multiply(rows, w_ref, outs):
    half = w_ref.shape[1] // 2
    blocks = len(outs) // 2
    for h in range(2):
        product = jnp.dot(
            rows, w_ref[:, h * half : (h + 1) * half], preferred_element_type=F32
        ).astype(BF16)
        for k in range(blocks):
            outs[h * blocks + k][...] = product[k * TOKENS_Z : (k + 1) * TOKENS_Z, :]


def far_kernel(*refs):
    pieces, w_ref, normed_ref, outs = refs[:8], refs[8], refs[9], refs[10:]
    for core_shift in range(2):
        for i in range(4):
            for p in range(4):
                rows = pl.ds(gathered_row(core_shift, i, p), TOKENS_OWN)
                normed_ref[rows, :] = pieces[core_shift * 4 + i][
                    p * TOKENS_OWN : (p + 1) * TOKENS_OWN, :
                ]
    multiply(normed_ref[HALF:, :], w_ref, outs)


def near_kernel(normed_ref, w_ref, *outs):
    multiply(normed_ref[:HALF, :], w_ref, outs)


def far_pre(pieces, weight):
    depth, width = weight.shape
    return pl.pallas_call(
        far_kernel,
        in_specs=[WHOLE] * 9,
        out_specs=[WHOLE] * 9,
        out_shape=[jax.ShapeDtypeStruct((TOKENS, depth), BF16)]
        + [jax.ShapeDtypeStruct((TOKENS_Z, width // 2), BF16)] * 8,
        **settings(weight, 16),
    )(*pieces, weight)


def near_pre(normed, weight):
    return pl.pallas_call(
        near_kernel,
        in_specs=[WHOLE] * 2,
        out_specs=[WHOLE] * 8,
        out_shape=[jax.ShapeDtypeStruct((TOKENS_Z, weight.shape[1] // 2), BF16)] * 8,
        **settings(weight, 16),
    )(normed, weight)


def transposed_dot(rows, weight):
    return lax.dot_general(rows, weight, (((1,), (1,)), ((), ())), preferred_element_type=F32)


def fill(rows_ref, pieces, blocks):
    half = rows_ref.shape[1] // 2
    for h in range(2):
        for k in range(blocks):
            rows_ref[
                k * TOKENS_Z : (k + 1) * TOKENS_Z, h * half : (h + 1) * half
            ] = pieces[h * blocks + k][...]


def near_back_kernel(*refs):
    pieces, w_ref, out_ref, rows_ref = refs[:8], refs[8], refs[9], refs[10]
    fill(rows_ref, pieces, 4)
    rows = rows_ref[...]
    for start in range(0, w_ref.shape[0], TILE):
        part = slice(start, start + TILE)
        out_ref[:, part] = transposed_dot(rows, w_ref[part, :]).astype(out_ref.dtype)


def near_back(pieces, weight):
    return pl.pallas_call(
        near_back_kernel,
        in_specs=[WHOLE] * 9,
        out_specs=WHOLE,
        out_shape=jax.ShapeDtypeStruct((HALF, weight.shape[0]), BF16),
        scratch_shapes=[pltpu.VMEM((HALF, weight.shape[1]), BF16)],
        **settings(weight, 16),
    )(*pieces, weight)


def far_back_kernel(*refs):
    pieces, near_ref, w_ref, slopes_ref, outs, product = (
        refs[:16], refs[16], refs[17], refs[18], refs[19:27], refs[27]
    )
    fill(slopes_ref, pieces, NZ)
    product[:HALF, :] = near_ref[...].astype(F32)
    rows = slopes_ref[HALF:, :]
    for start in range(0, w_ref.shape[0], TILE):
        part = slice(start, start + TILE)
        product[HALF:, part] = transposed_dot(rows, w_ref[part, :])
    for core_shift in (1, 0):
        for i in range(4):
            for p in range(4):
                outs[core_shift * 4 + i][p * TOKENS_OWN : (p + 1) * TOKENS_OWN, :] = product[
                    pl.ds(summed_row(core_shift, i, p), TOKENS_OWN), :
                ].astype(BF16)


def far_back(pieces, near, weight):
    depth, width = weight.shape
    return pl.pallas_call(
        far_back_kernel,
        in_specs=[WHOLE] * 18,
        out_specs=[WHOLE] * 9,
        out_shape=[jax.ShapeDtypeStruct((TOKENS, width), BF16)]
        + [jax.ShapeDtypeStruct((TOKENS_Z, depth), BF16)] * 8,
        scratch_shapes=[pltpu.VMEM((TOKENS, depth), F32)],
        **settings(weight, 16),
    )(*pieces, near, weight)


def gelu_tanh(value):
    return jax.nn.gelu(value, approximate=True)


def add(*values):
    total = values[0].astype(F32)
    for value in values[1:]:
        total = total + value.astype(F32)
    return total


def normalize(inputs, gain, bias):
    local = inputs.shape[1]
    local_mean = jnp.sum(inputs, axis=1) / local
    centered = inputs - local_mean[:, None]
    local_square = jnp.sum(centered * centered, axis=1)
    stats = jnp.stack([local_mean, local_square])
    every = lax.all_to_all(jnp.broadcast_to(stats[None], (NZ,) + stats.shape), "col", 0, 0)
    mean = jnp.mean(every[:, 0, :], axis=0)
    offset = every[:, 0, :] - mean[None, :]
    spread = (jnp.sum(every[:, 1, :], axis=0) + local * jnp.sum(offset * offset, axis=0)) / D
    scale = lax.rsqrt(spread + 1e-05)
    moved = centered + (local_mean - mean)[:, None]
    return (moved * scale[:, None] * gain[None, :] + bias[None, :]).astype(BF16)


def reduce_chain(parts):
    travelling = send_ring(parts[0], 1)
    for step, part in enumerate(parts[1:]):
        travelling = send_ring(add(part, travelling).astype(BF16), 2 * (step % 2) - 1)
    return travelling


def gather_chain(own, way, count):
    got = []
    for _ in range(count):
        own = send_ring(own, way)
        way = -way
        got.append(own)
    return got


def per_device(inputs, gain, bias, weight, d_act):
    normed = normalize(inputs, gain, bias)

    along_x = jnp.concatenate([normed] + [send_x(normed, s) for s in GATHER_X[1:]])
    along_y = [along_x] + [send_y(along_x, s) for s in GATHER_Y[1:]]
    weight, _ = lax.optimization_barrier((weight, along_x))
    along_y[3], weight = lax.optimization_barrier((along_y[3], stage(weight)))
    other = [send_core(v) for v in along_y]

    gathered, *far = far_pre(along_y + other, weight)
    near = near_pre(gathered, weight)
    half = weight.shape[1] // 2
    d_halves = lax.optimization_barrier((d_act[:, :half], d_act[:, half:]))
    pres, pieces, nearest = [], [], []
    for h in range(2):
        three, four, five, six = far[4 * h : 4 * h + 4]
        back, own, one, two = near[4 * h : 4 * h + 4]
        longer = reduce_chain([four, five, two, back])
        shorter = reduce_chain([three, six, one])
        pre = add(own, longer, shorter)
        slopes = jax.vjp(gelu_tanh, pre)[1](d_halves[h].astype(F32))[0].astype(BF16)
        block_1, block_6, block_3, block_4 = gather_chain(slopes, 1, 4)
        block_7, block_2, block_5 = gather_chain(slopes, -1, 3)
        nearest += [block_7, slopes, block_1, block_2]
        pieces += [block_7, slopes, block_1, block_2, block_3, block_4, block_5, block_6]
        pres.append(lax.optimization_barrier((pre, block_1))[0])
    activated = jnp.concatenate([gelu_tanh(pre).astype(BF16) for pre in pres], axis=1)

    near = near_back(nearest, weight)
    slopes_all, *parts = far_back(pieces, near, weight)
    d_weight = lax.dot_general(
        gathered, slopes_all, (((0,), (0,)), ((), ())), preferred_element_type=F32
    ).astype(BF16)

    sums = [add(parts[i], send_core(parts[4 + i])) for i in range(4)]
    arrived = [send_plane(sums[i].astype(BF16), SUM[i], 1) for i in range(1, 4)]
    line = add(sums[0], *arrived)
    line, d_weight = lax.optimization_barrier((line, d_weight))
    blocks = [line[i * TOKENS_OWN : (i + 1) * TOKENS_OWN] for i in range(4)]
    arrived = [send_plane(blocks[i].astype(BF16), SUM[i], 0) for i in range(1, 4)]
    d_normed = add(blocks[0], *arrived).astype(BF16)
    return (activated, d_normed, d_weight)


def solution(mesh):
    return jax.shard_map(
        per_device,
        mesh=mesh,
        in_specs=(P("row", "col"), P("col"), P("col"), P("col", "row"), P("col", "row")),
        out_specs=(P("col", "row"), P("row", "col"), P("col", "row")),
        check_vma=False,
    )
```

```python
import jax
import jax.numpy as jnp
from jax import lax
from jax.experimental import pallas as pl
from jax.experimental.pallas import tpu as pltpu
from jax.sharding import PartitionSpec as P

D = 12288
F32, BF16 = jnp.float32, jnp.bfloat16

NX, NY, NC, NZ = 4, 4, 2, 8
GATHER_X, GATHER_Y, SUM_FIRST, SUM_LAST = (0, 1, 3, 2), (0, 2, 3, 1), (0, 1, 3, 2), (0, 3, 1, 2)
TOKENS_OWN = 16
TOKENS_Z = 64
TOKENS = 512
HALF = TOKENS // 2


def pairs_of(target):
    pairs = []
    for x in range(NX):
        for y in range(NY):
            for c in range(NC):
                for z in range(NZ):
                    source = ((x * NY + y) * NC + c) * NZ + z
                    tx, ty, tc, tz = target(x, y, c, z)
                    place = ((tx % NX) * NY + ty % NY) * NC + tc % NC
                    pairs.append((source, place * NZ + tz % NZ))
    return pairs


def send(value, target):
    return lax.ppermute(value, ("row", "col"), pairs_of(target))


def send_x(value, k):
    return send(value, lambda x, y, c, z: (x ^ k, y, c, z))


def send_y(value, shift):
    return send(value, lambda x, y, c, z: (x, y + shift, c, z))


def send_plane(value, k, x_core):
    return send(value, lambda x, y, c, z: (x ^ k, y, c, z) if c == x_core else (x, y ^ k, c, z))


def send_core(value):
    return send(value, lambda x, y, c, z: (x, y, c + 1, z))


def send_ring(value, way):
    return send(value, lambda x, y, c, z: (x, y, c, z + way * (1 - 2 * ((z + c) % 2))))


def row_of(block):
    row, col = lax.axis_index("row"), lax.axis_index("col")
    own = TOKENS_Z // TOKENS_OWN
    place = ((block // own - col) * (1 - 2 * ((row + col) % 2)) + 1 + 2 * NZ) % NZ
    return pl.multiple_of(place * TOKENS_Z + (block % own) * TOKENS_OWN, TOKENS_OWN)


def gathered_row(core_shift, i, p):
    row = lax.axis_index("row")
    x, y, c = row // (NY * NC), (row // NC) % NY, row % NC
    x, y = x ^ GATHER_X[p], (y + NY - GATHER_Y[i]) % NY
    return row_of((x * NY + y) * NC + (c + core_shift) % NC)


def summed_row(core_shift, i, p):
    row = lax.axis_index("row")
    x, y, c = row // (NY * NC), (row // NC) % NY, row % NC
    core = (c + core_shift) % NC
    x = x ^ jnp.where(core == 1, SUM_FIRST[i], SUM_LAST[p])
    y = y ^ jnp.where(core == 1, SUM_LAST[p], SUM_FIRST[i])
    return row_of((x * NY + y) * NC + core)


WHOLE = pl.BlockSpec(memory_space=pltpu.VMEM)
TILE = 512


def settings(weight, limit):
    depth, width = weight.shape
    return dict(
        compiler_params=pltpu.CompilerParams(vmem_limit_bytes=limit << 20),
        cost_estimate=pl.CostEstimate(
            flops=TOKENS * depth * width, bytes_accessed=depth * width * 2, transcendentals=0
        ),
    )


def stage_kernel(w_ref, out_ref, sem):
    copy = pltpu.make_async_copy(w_ref, out_ref, sem)
    copy.start()
    copy.wait()


def stage(weight):
    return pl.pallas_call(
        stage_kernel,
        in_specs=[pl.BlockSpec(memory_space=pl.ANY)],
        out_specs=WHOLE,
        out_shape=jax.ShapeDtypeStruct(weight.shape, weight.dtype),
        scratch_shapes=[pltpu.SemaphoreType.DMA],
        **settings(weight, 48),
    )(weight)


def multiply(rows, w_ref, outs):
    half = w_ref.shape[1] // 2
    for h in range(2):
        columns = slice(h * half, (h + 1) * half)
        product = jnp.dot(rows, w_ref[:, columns], preferred_element_type=F32).astype(BF16)
        for k, out in enumerate(outs):
            block = product[k * TOKENS_Z : (k + 1) * TOKENS_Z, :]
            if len(out) == 2:
                out[h][...] = block
            else:
                out[0][:, columns] = block


def halves_of(cut, refs):
    refs = list(refs)
    return [[refs.pop(0) for _ in range(1 + flag)] for flag in cut]


def shapes_of(cut, width):
    return [
        jax.ShapeDtypeStruct((TOKENS_Z, width // (1 + flag)), BF16)
        for flag in cut
        for _ in range(1 + flag)
    ]


SUM_CUT = (1, 0, 0, 1, 0, 1, 1, 0)
GATHER_CUT = (0, 0, 1, 0, 1, 1, 0, 1)


def far_kernel(*refs):
    pieces, w_ref, normed_ref, outs = refs[:8], refs[8], refs[9], refs[10:]
    for core_shift in range(2):
        for i in range(4):
            for p in range(4):
                rows = pl.ds(gathered_row(core_shift, i, p), TOKENS_OWN)
                normed_ref[rows, :] = pieces[core_shift * 4 + i][
                    p * TOKENS_OWN : (p + 1) * TOKENS_OWN, :
                ]
    multiply(normed_ref[HALF:, :], w_ref, halves_of(SUM_CUT[4:], outs))


def near_kernel(normed_ref, w_ref, *outs):
    multiply(normed_ref[:HALF, :], w_ref, halves_of(SUM_CUT[:4], outs))


def far_pre(pieces, weight):
    depth, width = weight.shape
    return pl.pallas_call(
        far_kernel,
        in_specs=[WHOLE] * 9,
        out_specs=[WHOLE] * (5 + sum(SUM_CUT[4:])),
        out_shape=[jax.ShapeDtypeStruct((TOKENS, depth), BF16)] + shapes_of(SUM_CUT[4:], width),
        **settings(weight, 16),
    )(*pieces, weight)


def near_pre(normed, weight):
    return pl.pallas_call(
        near_kernel,
        in_specs=[WHOLE] * 2,
        out_specs=[WHOLE] * (4 + sum(SUM_CUT[:4])),
        out_shape=shapes_of(SUM_CUT[:4], weight.shape[1]),
        **settings(weight, 16),
    )(normed, weight)


def transposed_dot(rows, weight):
    return lax.dot_general(rows, weight, (((1,), (1,)), ((), ())), preferred_element_type=F32)


def fill(rows_ref, blocks):
    half = rows_ref.shape[1] // 2
    for k, block in enumerate(blocks):
        rows = slice(k * TOKENS_Z, (k + 1) * TOKENS_Z)
        if len(block) == 2:
            rows_ref[rows, :half] = block[0][...]
            rows_ref[rows, half:] = block[1][...]
        else:
            rows_ref[rows, :] = block[0][...]


def near_back_kernel(*refs):
    *pieces, w_ref, out_ref, rows_ref = refs
    fill(rows_ref, halves_of(GATHER_CUT[:4], pieces))
    rows = rows_ref[...]
    for start in range(0, w_ref.shape[0], TILE):
        part = slice(start, start + TILE)
        out_ref[:, part] = transposed_dot(rows, w_ref[part, :]).astype(out_ref.dtype)


def near_back(pieces, weight):
    return pl.pallas_call(
        near_back_kernel,
        in_specs=[WHOLE] * (len(pieces) + 1),
        out_specs=WHOLE,
        out_shape=jax.ShapeDtypeStruct((HALF, weight.shape[0]), BF16),
        scratch_shapes=[pltpu.VMEM((HALF, weight.shape[1]), BF16)],
        **settings(weight, 16),
    )(*pieces, weight)


def far_back_kernel(*refs):
    *pieces, near_ref, w_ref, slopes_ref = refs[:-9]
    outs, product = refs[-9:-1], refs[-1]
    fill(slopes_ref, halves_of(GATHER_CUT, pieces))
    product[:HALF, :] = near_ref[...].astype(F32)
    rows = slopes_ref[HALF:, :]
    for start in range(0, w_ref.shape[0], TILE):
        part = slice(start, start + TILE)
        product[HALF:, part] = transposed_dot(rows, w_ref[part, :])
    for core_shift in (1, 0):
        for i in range(4):
            for p in range(4):
                outs[core_shift * 4 + i][p * TOKENS_OWN : (p + 1) * TOKENS_OWN, :] = product[
                    pl.ds(summed_row(core_shift, i, p), TOKENS_OWN), :
                ].astype(BF16)


def far_back(pieces, near, weight):
    depth, width = weight.shape
    return pl.pallas_call(
        far_back_kernel,
        in_specs=[WHOLE] * (len(pieces) + 2),
        out_specs=[WHOLE] * 9,
        out_shape=[jax.ShapeDtypeStruct((TOKENS, width), BF16)]
        + [jax.ShapeDtypeStruct((TOKENS_Z, depth), BF16)] * 8,
        scratch_shapes=[pltpu.VMEM((TOKENS, depth), F32)],
        **settings(weight, 16),
    )(*pieces, near, weight)


def gelu_tanh(value):
    return jax.nn.gelu(value, approximate=True)


def add(*values):
    total = values[0].astype(F32)
    for value in values[1:]:
        total = total + value.astype(F32)
    return total


def normalize(inputs, gain, bias):
    local = inputs.shape[1]
    local_mean = jnp.sum(inputs, axis=1) / local
    centered = inputs - local_mean[:, None]
    local_square = jnp.sum(centered * centered, axis=1)
    stats = jnp.stack([local_mean, local_square])
    every = lax.all_to_all(jnp.broadcast_to(stats[None], (NZ,) + stats.shape), "col", 0, 0)
    mean = jnp.mean(every[:, 0, :], axis=0)
    offset = every[:, 0, :] - mean[None, :]
    spread = (jnp.sum(every[:, 1, :], axis=0) + local * jnp.sum(offset * offset, axis=0)) / D
    scale = lax.rsqrt(spread + 1e-05)
    moved = centered + (local_mean - mean)[:, None]
    return (moved * scale[:, None] * gain[None, :] + bias[None, :]).astype(BF16)


def reduce_chain(parts):
    travelling = send_ring(parts[0], 1)
    for step, part in enumerate(parts[1:]):
        travelling = send_ring(add(part, travelling).astype(BF16), 2 * (step % 2) - 1)
    return travelling


def gather_chain(own, way, count):
    got = []
    for _ in range(count):
        own = send_ring(own, way)
        way = -way
        got.append(own)
    return got


def per_device(inputs, gain, bias, weight, d_act):
    normed = normalize(inputs, gain, bias)

    along_x = jnp.concatenate([normed] + [send_x(normed, s) for s in GATHER_X[1:]])
    along_y = [along_x] + [send_y(along_x, s) for s in GATHER_Y[1:]]
    weight, _ = lax.optimization_barrier((weight, along_x))
    along_y[3], weight = lax.optimization_barrier((along_y[3], stage(weight)))
    other = [send_core(v) for v in along_y]

    gathered, *far = far_pre(along_y + other, weight)
    three, four, five, six = halves_of(SUM_CUT[4:], far)
    back, own, one, two = halves_of(SUM_CUT[:4], near_pre(gathered, weight))
    longer = [reduce_chain([four[h], five[h], two[h], back[h]]) for h in range(2)]
    shorter = reduce_chain([three[0], six[0], one[0]])
    pre = add(own[0], jnp.concatenate(longer, axis=1), shorter)
    slopes = jax.vjp(gelu_tanh, pre)[1](d_act.astype(F32))[0].astype(BF16)

    half = weight.shape[1] // 2
    longer = [gather_chain(slopes[:, h * half : (h + 1) * half], 1, 4) for h in range(2)]
    block_1, block_6, block_3, block_4 = ([chain[i] for chain in longer] for i in range(4))
    block_7, block_2, block_5 = ([v] for v in gather_chain(slopes, -1, 3))
    nearest = block_7 + [slopes] + block_1 + block_2
    pieces = nearest + block_3 + block_4 + block_5 + block_6
    pre, _ = lax.optimization_barrier((pre, block_4[0]))
    activated = gelu_tanh(pre).astype(BF16)

    near = near_back(nearest, weight)
    slopes_all, *parts = far_back(pieces, near, weight)
    d_weight = lax.dot_general(
        gathered, slopes_all, (((0,), (0,)), ((), ())), preferred_element_type=F32
    ).astype(BF16)

    sums = [add(parts[i], send_core(parts[4 + i])) for i in range(4)]
    arrived = [send_plane(sums[i].astype(BF16), SUM_FIRST[i], 1) for i in range(1, 4)]
    line = add(sums[0], *arrived)
    line, d_weight = lax.optimization_barrier((line, d_weight))
    blocks = [line[i * TOKENS_OWN : (i + 1) * TOKENS_OWN] for i in range(4)]
    arrived = [send_plane(blocks[i].astype(BF16), SUM_LAST[i], 0) for i in range(1, 4)]
    d_normed = add(blocks[0], *arrived).astype(BF16)
    return (activated, d_normed, d_weight)


def solution(mesh):
    return jax.shard_map(
        per_device,
        mesh=mesh,
        in_specs=(P("row", "col"), P("col"), P("col"), P("col", "row"), P("col", "row")),
        out_specs=(P("col", "row"), P("row", "col"), P("col", "row")),
        check_vma=False,
    )
```

```python
import jax
import jax.numpy as jnp
from jax import lax
from jax.experimental import pallas as pl
from jax.experimental.pallas import tpu as pltpu
from jax.sharding import PartitionSpec as P

D = 12288
F32, BF16 = jnp.float32, jnp.bfloat16

NX, NY, NC, NZ = 4, 4, 2, 8
GATHER_X, GATHER_Y, SUM_FIRST, SUM_LAST = (0, 1, 3, 2), (0, 1, 2, 3), (0, 3, 2, 1), (0, 3, 1, 2)
TOKENS_OWN = 16
TOKENS_Z = 64
TOKENS = 512
HALF = TOKENS // 2


def pairs_of(target):
    pairs = []
    for x in range(NX):
        for y in range(NY):
            for c in range(NC):
                for z in range(NZ):
                    source = ((x * NY + y) * NC + c) * NZ + z
                    tx, ty, tc, tz = target(x, y, c, z)
                    place = ((tx % NX) * NY + ty % NY) * NC + tc % NC
                    pairs.append((source, place * NZ + tz % NZ))
    return pairs


def send(value, target):
    return lax.ppermute(value, ("row", "col"), pairs_of(target))


def send_x(value, k):
    return send(value, lambda x, y, c, z: (x ^ k, y, c, z))


def send_y(value, k):
    return send(value, lambda x, y, c, z: (x, y ^ k, c, z))


def send_plane(value, k, x_core):
    return send(value, lambda x, y, c, z: (x ^ k, y, c, z) if c == x_core else (x, y ^ k, c, z))


def send_core(value):
    return send(value, lambda x, y, c, z: (x, y, c + 1, z))


def send_ring(value, way):
    return send(value, lambda x, y, c, z: (x, y, c, z + way * (1 - 2 * ((z + c) % 2))))


def row_of(block):
    row, col = lax.axis_index("row"), lax.axis_index("col")
    own = TOKENS_Z // TOKENS_OWN
    place = ((block // own - col) * (1 - 2 * ((row + col) % 2)) + 1 + 2 * NZ) % NZ
    return pl.multiple_of(place * TOKENS_Z + (block % own) * TOKENS_OWN, TOKENS_OWN)


def gathered_row(core_shift, i, p):
    row = lax.axis_index("row")
    x, y, c = row // (NY * NC), (row // NC) % NY, row % NC
    x, y = x ^ GATHER_X[p], y ^ GATHER_Y[i]
    return row_of((x * NY + y) * NC + (c + core_shift) % NC)


def summed_row(core_shift, i, p):
    row = lax.axis_index("row")
    x, y, c = row // (NY * NC), (row // NC) % NY, row % NC
    core = (c + core_shift) % NC
    x = x ^ jnp.where(core == 1, SUM_FIRST[i], SUM_LAST[p])
    y = y ^ jnp.where(core == 1, SUM_LAST[p], SUM_FIRST[i])
    return row_of((x * NY + y) * NC + core)


WHOLE = pl.BlockSpec(memory_space=pltpu.VMEM)
TILE = 512


def settings(weight, limit):
    depth, width = weight.shape
    return dict(
        compiler_params=pltpu.CompilerParams(vmem_limit_bytes=limit << 20),
        cost_estimate=pl.CostEstimate(
            flops=TOKENS * depth * width, bytes_accessed=depth * width * 2, transcendentals=0
        ),
    )


def stage_kernel(w_ref, out_ref, sem):
    copy = pltpu.make_async_copy(w_ref, out_ref, sem)
    copy.start()
    copy.wait()


def stage(weight):
    return pl.pallas_call(
        stage_kernel,
        in_specs=[pl.BlockSpec(memory_space=pl.ANY)],
        out_specs=WHOLE,
        out_shape=jax.ShapeDtypeStruct(weight.shape, weight.dtype),
        scratch_shapes=[pltpu.SemaphoreType.DMA],
        **settings(weight, 48),
    )(weight)


def multiply(rows, w_ref, outs):
    half = w_ref.shape[1] // 2
    for h in range(2):
        columns = slice(h * half, (h + 1) * half)
        product = jnp.dot(rows, w_ref[:, columns], preferred_element_type=F32).astype(BF16)
        for k, out in enumerate(outs):
            block = product[k * TOKENS_Z : (k + 1) * TOKENS_Z, :]
            if len(out) == 2:
                out[h][...] = block
            else:
                out[0][:, columns] = block


def halves_of(cut, refs):
    refs = list(refs)
    return [[refs.pop(0) for _ in range(1 + flag)] for flag in cut]


def shapes_of(cut, width):
    return [
        jax.ShapeDtypeStruct((TOKENS_Z, width // (1 + flag)), BF16)
        for flag in cut
        for _ in range(1 + flag)
    ]


CUT = (1, 0, 0, 1, 0, 1, 1, 0)


def far_kernel(*refs):
    pieces, w_ref, normed_ref, outs = refs[:8], refs[8], refs[9], refs[10:]
    for core_shift in range(2):
        for i in range(4):
            for p in range(4):
                rows = pl.ds(gathered_row(core_shift, i, p), TOKENS_OWN)
                normed_ref[rows, :] = pieces[core_shift * 4 + i][
                    p * TOKENS_OWN : (p + 1) * TOKENS_OWN, :
                ]
    multiply(normed_ref[HALF:, :], w_ref, halves_of(CUT[4:], outs))


def near_kernel(normed_ref, w_ref, *outs):
    multiply(normed_ref[:HALF, :], w_ref, halves_of(CUT[:4], outs))


def far_pre(pieces, weight):
    depth, width = weight.shape
    return pl.pallas_call(
        far_kernel,
        in_specs=[WHOLE] * 9,
        out_specs=[WHOLE] * (5 + sum(CUT[4:])),
        out_shape=[jax.ShapeDtypeStruct((TOKENS, depth), BF16)] + shapes_of(CUT[4:], width),
        **settings(weight, 16),
    )(*pieces, weight)


def near_pre(normed, weight):
    return pl.pallas_call(
        near_kernel,
        in_specs=[WHOLE] * 2,
        out_specs=[WHOLE] * (4 + sum(CUT[:4])),
        out_shape=shapes_of(CUT[:4], weight.shape[1]),
        **settings(weight, 16),
    )(normed, weight)


def transposed_dot(rows, weight):
    return lax.dot_general(rows, weight, (((1,), (1,)), ((), ())), preferred_element_type=F32)


def fill(rows_ref, blocks):
    half = rows_ref.shape[1] // 2
    for k, block in enumerate(blocks):
        rows = slice(k * TOKENS_Z, (k + 1) * TOKENS_Z)
        if len(block) == 2:
            rows_ref[rows, :half] = block[0][...]
            rows_ref[rows, half:] = block[1][...]
        else:
            rows_ref[rows, :] = block[0][...]


def near_back_kernel(*refs):
    *pieces, w_ref, out_ref, rows_ref = refs
    fill(rows_ref, halves_of(CUT[:4], pieces))
    rows = rows_ref[...]
    for start in range(0, w_ref.shape[0], TILE):
        part = slice(start, start + TILE)
        out_ref[:, part] = transposed_dot(rows, w_ref[part, :]).astype(out_ref.dtype)


def near_back(pieces, weight):
    return pl.pallas_call(
        near_back_kernel,
        in_specs=[WHOLE] * (len(pieces) + 1),
        out_specs=WHOLE,
        out_shape=jax.ShapeDtypeStruct((HALF, weight.shape[0]), BF16),
        scratch_shapes=[pltpu.VMEM((HALF, weight.shape[1]), BF16)],
        **settings(weight, 16),
    )(*pieces, weight)


def far_back_kernel(*refs):
    *pieces, near_ref, w_ref, slopes_ref = refs[:-9]
    outs, product = refs[-9:-1], refs[-1]
    fill(slopes_ref, halves_of(CUT, pieces))
    product[:HALF, :] = near_ref[...].astype(F32)
    rows = slopes_ref[HALF:, :]
    for start in range(0, w_ref.shape[0], TILE):
        part = slice(start, start + TILE)
        product[HALF:, part] = transposed_dot(rows, w_ref[part, :])
    for core_shift in (1, 0):
        for i in range(4):
            for p in range(4):
                outs[core_shift * 4 + i][p * TOKENS_OWN : (p + 1) * TOKENS_OWN, :] = product[
                    pl.ds(summed_row(core_shift, i, p), TOKENS_OWN), :
                ].astype(BF16)


def far_back(pieces, near, weight):
    depth, width = weight.shape
    return pl.pallas_call(
        far_back_kernel,
        in_specs=[WHOLE] * (len(pieces) + 2),
        out_specs=[WHOLE] * 9,
        out_shape=[jax.ShapeDtypeStruct((TOKENS, width), BF16)]
        + [jax.ShapeDtypeStruct((TOKENS_Z, depth), BF16)] * 8,
        scratch_shapes=[pltpu.VMEM((TOKENS, depth), F32)],
        **settings(weight, 16),
    )(*pieces, near, weight)


def gelu_tanh(value):
    return jax.nn.gelu(value, approximate=True)


def add(*values):
    total = values[0].astype(F32)
    for value in values[1:]:
        total = total + value.astype(F32)
    return total


LANES = 128


def center_kernel(*refs):
    sources, (centered_ref, stats_ref, *vectors), sems = refs[:3], refs[3:7], refs[7]
    copies = [
        pltpu.make_async_copy(source, target, sems.at[i])
        for i, (source, target) in enumerate(zip(sources, [centered_ref] + vectors))
    ]
    for copy in copies:
        copy.start()
    copies[0].wait()
    rows = centered_ref[...]
    mean = jnp.sum(rows, axis=1, keepdims=True) / rows.shape[1]
    centered = rows - mean
    centered_ref[...] = centered
    square = jnp.sum(centered * centered, axis=1, keepdims=True)
    lane = lax.broadcasted_iota(jnp.int32, (rows.shape[0], LANES), 1)
    stats = jnp.where(lane < LANES // 2, mean, square)
    for k in range(NZ):
        stats_ref[k] = stats
    for copy in copies[1:]:
        copy.wait()


def scale_kernel(centered_ref, own_ref, every_ref, gain_ref, bias_ref, normed_ref):
    centered = centered_ref[...]
    local = centered.shape[1]
    means = [every_ref[k][:, :1] for k in range(NZ)]
    squares = [every_ref[k][:, LANES // 2 : LANES // 2 + 1] for k in range(NZ)]
    mean = sum(means) / NZ
    spread = sum(square + local * (m - mean) * (m - mean) for m, square in zip(means, squares))
    scale = lax.rsqrt(spread / D + 1e-05)
    moved = centered + (own_ref[0][:, :1] - mean)
    normed_ref[...] = (moved * scale * gain_ref[...][None, :] + bias_ref[...][None, :]).astype(BF16)


def normalize(inputs, gain, bias):
    rows = inputs.shape[0]
    centered, own, gain, bias = pl.pallas_call(
        center_kernel,
        in_specs=[pl.BlockSpec(memory_space=pl.ANY)] * 3,
        out_specs=[WHOLE] * 4,
        out_shape=[
            jax.ShapeDtypeStruct(inputs.shape, F32),
            jax.ShapeDtypeStruct((NZ, rows, LANES), F32),
            jax.ShapeDtypeStruct(gain.shape, F32),
            jax.ShapeDtypeStruct(bias.shape, F32),
        ],
        scratch_shapes=[pltpu.SemaphoreType.DMA((3,))],
        compiler_params=pltpu.CompilerParams(vmem_limit_bytes=60 << 20),
    )(inputs, gain, bias)
    every = lax.all_to_all(own, "col", 0, 0)
    return pl.pallas_call(
        scale_kernel,
        in_specs=[WHOLE] * 5,
        out_specs=WHOLE,
        out_shape=jax.ShapeDtypeStruct(inputs.shape, BF16),
    )(centered, own, every, gain, bias)


def reduce_chain(parts):
    travelling = send_ring(parts[0], 1)
    for step, part in enumerate(parts[1:]):
        travelling = send_ring(add(part, travelling).astype(BF16), 2 * (step % 2) - 1)
    return travelling


def gather_chain(own, way, count):
    got = []
    for _ in range(count):
        own = send_ring(own, way)
        way = -way
        got.append(own)
    return got


def per_device(inputs, gain, bias, weight, d_act):
    normed = normalize(inputs, gain, bias)

    along_x = jnp.concatenate([normed] + [send_x(normed, s) for s in GATHER_X[1:]])
    along_y = [along_x] + [send_y(along_x, s) for s in GATHER_Y[1:]]
    weight, _ = lax.optimization_barrier((weight, along_x))
    along_y[3], weight = lax.optimization_barrier((along_y[3], stage(weight)))
    other = [send_core(v) for v in along_y]

    gathered, *far = far_pre(along_y + other, weight)
    three, four, five, six = halves_of(CUT[4:], far)
    back, own, one, two = halves_of(CUT[:4], near_pre(gathered, weight))
    longer = [reduce_chain([four[h], five[h], two[h], back[h]]) for h in range(2)]
    shorter = reduce_chain([three[0], six[0], one[0]])
    pre = add(own[0], jnp.concatenate(longer, axis=1), shorter)
    slopes = jax.vjp(gelu_tanh, pre)[1](d_act.astype(F32))[0].astype(BF16)

    half = weight.shape[1] // 2
    slopes, *cut = lax.optimization_barrier((slopes, slopes[:, :half], slopes[:, half:]))
    longer = [gather_chain(part, -1, 4) for part in cut]
    block_7, block_2, block_5, block_4 = ([chain[i] for chain in longer] for i in range(4))
    block_1, block_6, block_3 = ([v] for v in gather_chain(slopes, 1, 3))
    nearest = block_7 + [slopes] + block_1 + block_2
    pieces = nearest + block_3 + block_4 + block_5 + block_6
    pre, _ = lax.optimization_barrier((pre, block_4[0]))
    activated = gelu_tanh(pre).astype(BF16)

    near = near_back(nearest, weight)
    slopes_all, *parts = far_back(pieces, near, weight)
    d_weight = lax.dot_general(
        gathered, slopes_all, (((0,), (0,)), ((), ())), preferred_element_type=F32
    ).astype(BF16)

    sums = [add(parts[i], send_core(parts[4 + i])) for i in range(4)]
    arrived = [send_plane(sums[i].astype(BF16), SUM_FIRST[i], 1) for i in range(1, 4)]
    line = add(sums[0], *arrived)
    line, d_weight = lax.optimization_barrier((line, d_weight))
    blocks = [line[i * TOKENS_OWN : (i + 1) * TOKENS_OWN] for i in range(4)]
    arrived = [send_plane(blocks[i].astype(BF16), SUM_LAST[i], 0) for i in range(1, 4)]
    d_normed = add(blocks[0], *arrived).astype(BF16)
    return (activated, d_normed, d_weight)


def solution(mesh):
    return jax.shard_map(
        per_device,
        mesh=mesh,
        in_specs=(P("row", "col"), P("col"), P("col"), P("col", "row"), P("col", "row")),
        out_specs=(P("col", "row"), P("row", "col"), P("col", "row")),
        check_vma=False,
    )
```

```python
import functools

import jax
import jax.numpy as jnp
from jax import lax
from jax.experimental import pallas as pl
from jax.experimental.pallas import tpu as pltpu
from jax.sharding import PartitionSpec as P

D = 12288
F32, BF16 = jnp.float32, jnp.bfloat16

NX, NY, NC, NZ = 4, 4, 2, 8
GATHER_X, GATHER_Y, SUM_FIRST, SUM_LAST = (0, 1, 3, 2), (0, 1, 2, 3), (0, 3, 2, 1), (0, 3, 1, 2)
TOKENS_OWN = 16
TOKENS_Z = 64
TOKENS = 512


def pairs_of(target):
    pairs = []
    for x in range(NX):
        for y in range(NY):
            for c in range(NC):
                for z in range(NZ):
                    source = ((x * NY + y) * NC + c) * NZ + z
                    tx, ty, tc, tz = target(x, y, c, z)
                    place = ((tx % NX) * NY + ty % NY) * NC + tc % NC
                    pairs.append((source, place * NZ + tz % NZ))
    return pairs


def send(value, target):
    return lax.ppermute(value, ("row", "col"), pairs_of(target))


def send_x(value, k):
    return send(value, lambda x, y, c, z: (x ^ k, y, c, z))


def send_y(value, k):
    return send(value, lambda x, y, c, z: (x, y ^ k, c, z))


def send_plane(value, k, x_core):
    return send(value, lambda x, y, c, z: (x ^ k, y, c, z) if c == x_core else (x, y ^ k, c, z))


def send_core(value):
    return send(value, lambda x, y, c, z: (x, y, c + 1, z))


def send_ring(value, way):
    return send(value, lambda x, y, c, z: (x, y, c, z + way * (1 - 2 * ((z + c) % 2))))


def row_of(block):
    row, col = lax.axis_index("row"), lax.axis_index("col")
    own = TOKENS_Z // TOKENS_OWN
    place = ((block // own - col) * (1 - 2 * ((row + col) % 2)) + 1 + 2 * NZ) % NZ
    return pl.multiple_of(place * TOKENS_Z + (block % own) * TOKENS_OWN, TOKENS_OWN)


def gathered_row(core_shift, i, p):
    row = lax.axis_index("row")
    x, y, c = row // (NY * NC), (row // NC) % NY, row % NC
    x, y = x ^ GATHER_X[p], y ^ GATHER_Y[i]
    return row_of((x * NY + y) * NC + (c + core_shift) % NC)


def summed_row(core_shift, i, p):
    row = lax.axis_index("row")
    x, y, c = row // (NY * NC), (row // NC) % NY, row % NC
    core = (c + core_shift) % NC
    x = x ^ jnp.where(core == 1, SUM_FIRST[i], SUM_LAST[p])
    y = y ^ jnp.where(core == 1, SUM_LAST[p], SUM_FIRST[i])
    return row_of((x * NY + y) * NC + core)


WHOLE = pl.BlockSpec(memory_space=pltpu.VMEM)
TILE = 512


def settings(weight, limit):
    depth, width = weight.shape
    return dict(
        compiler_params=pltpu.CompilerParams(vmem_limit_bytes=limit << 20),
        cost_estimate=pl.CostEstimate(
            flops=TOKENS * depth * width, bytes_accessed=depth * width * 2, transcendentals=0
        ),
    )


def stage_kernel(w_ref, out_ref, sem):
    copy = pltpu.make_async_copy(w_ref, out_ref, sem)
    copy.start()
    copy.wait()


def stage(weight):
    return pl.pallas_call(
        stage_kernel,
        in_specs=[pl.BlockSpec(memory_space=pl.ANY)],
        out_specs=WHOLE,
        out_shape=jax.ShapeDtypeStruct(weight.shape, weight.dtype),
        scratch_shapes=[pltpu.SemaphoreType.DMA],
        **settings(weight, 48),
    )(weight)


def multiply(rows, w_ref, outs):
    half = w_ref.shape[1] // 2
    for h in range(2):
        columns = slice(h * half, (h + 1) * half)
        product = jnp.dot(rows, w_ref[:, columns], preferred_element_type=F32).astype(BF16)
        for k, out in enumerate(outs):
            block = product[k * TOKENS_Z : (k + 1) * TOKENS_Z, :]
            if len(out) == 2:
                out[h][...] = block
            else:
                out[0][:, columns] = block


def halves_of(cut, refs):
    refs = list(refs)
    return [[refs.pop(0) for _ in range(1 + flag)] for flag in cut]


def shapes_of(cut, width):
    return [
        jax.ShapeDtypeStruct((TOKENS_Z, width // (1 + flag)), BF16)
        for flag in cut
        for _ in range(1 + flag)
    ]


SUM_CUT = (1, 0, 0, 1, 0, 1, 1, 0)
FIRST, REST = (4, 6), (0, 4, 6, 8)
GATHER_CUT = (1, 0, 1, 1, 1, 1, 1, 1)


def z_rows(start, stop):
    return slice(start * TOKENS_Z, stop * TOKENS_Z)


def first_kernel(*refs):
    pieces, w_ref, normed_ref, outs = refs[:8], refs[8], refs[9], refs[10:]
    for core_shift in range(2):
        for i in range(4):
            for p in range(4):
                rows = pl.ds(gathered_row(core_shift, i, p), TOKENS_OWN)
                normed_ref[rows, :] = pieces[core_shift * 4 + i][
                    p * TOKENS_OWN : (p + 1) * TOKENS_OWN, :
                ]
    multiply(normed_ref[z_rows(*FIRST), :], w_ref, halves_of(SUM_CUT[slice(*FIRST)], outs))


def rest_kernel(normed_ref, w_ref, *outs):
    outs = list(outs)
    for part in (REST[:2], REST[2:]):
        cut = SUM_CUT[slice(*part)]
        count = len(cut) + sum(cut)
        multiply(normed_ref[z_rows(*part), :], w_ref, halves_of(cut, outs[:count]))
        outs = outs[count:]


def first_pre(pieces, weight):
    depth, width = weight.shape
    shapes = shapes_of(SUM_CUT[slice(*FIRST)], width)
    return pl.pallas_call(
        first_kernel,
        in_specs=[WHOLE] * 9,
        out_specs=[WHOLE] * (1 + len(shapes)),
        out_shape=[jax.ShapeDtypeStruct((TOKENS, depth), BF16)] + shapes,
        **settings(weight, 16),
    )(*pieces, weight)


def rest_pre(normed, weight):
    shapes = shapes_of(SUM_CUT[slice(*REST[:2])] + SUM_CUT[slice(*REST[2:])], weight.shape[1])
    return pl.pallas_call(
        rest_kernel,
        in_specs=[WHOLE] * 2,
        out_specs=[WHOLE] * len(shapes),
        out_shape=shapes,
        **settings(weight, 16),
    )(normed, weight)


def transposed_dot(rows, weight):
    return lax.dot_general(rows, weight, (((1,), (1,)), ((), ())), preferred_element_type=F32)


def fill(rows_ref, blocks):
    half = rows_ref.shape[1] // 2
    for k, block in enumerate(blocks):
        if len(block) == 2:
            rows_ref[z_rows(k, k + 1), :half] = block[0][...]
            rows_ref[z_rows(k, k + 1), half:] = block[1][...]
        else:
            rows_ref[z_rows(k, k + 1), :] = block[0][...]


def some_back_kernel(cut, *refs):
    *pieces, w_ref, out_ref, rows_ref = refs
    fill(rows_ref, halves_of(cut, pieces))
    rows = rows_ref[...]
    for start in range(0, w_ref.shape[0], TILE):
        part = slice(start, start + TILE)
        out_ref[:, part] = transposed_dot(rows, w_ref[part, :]).astype(out_ref.dtype)


def some_back(blocks, weight):
    cut = [len(block) - 1 for block in blocks]
    pieces = sum(blocks, [])
    rows = len(blocks) * TOKENS_Z
    return pl.pallas_call(
        functools.partial(some_back_kernel, cut),
        in_specs=[WHOLE] * (len(pieces) + 1),
        out_specs=WHOLE,
        out_shape=jax.ShapeDtypeStruct((rows, weight.shape[0]), BF16),
        scratch_shapes=[pltpu.VMEM((rows, weight.shape[1]), BF16)],
        **settings(weight, 16),
    )(*pieces, weight)


def last_back_kernel(*refs):
    *pieces, near_ref, middle_ref, w_ref, slopes_ref = refs[:-9]
    outs, product = refs[-9:-1], refs[-1]
    fill(slopes_ref, halves_of(GATHER_CUT, pieces))
    product[z_rows(0, 4), :] = near_ref[...].astype(F32)
    product[z_rows(4, 5), :] = middle_ref[z_rows(0, 1), :].astype(F32)
    product[z_rows(7, 8), :] = middle_ref[z_rows(1, 2), :].astype(F32)
    rows = slopes_ref[z_rows(5, 7), :]
    for start in range(0, w_ref.shape[0], TILE):
        part = slice(start, start + TILE)
        product[z_rows(5, 7), part] = transposed_dot(rows, w_ref[part, :])
    for core_shift in (1, 0):
        for i in range(4):
            for p in range(4):
                outs[core_shift * 4 + i][p * TOKENS_OWN : (p + 1) * TOKENS_OWN, :] = product[
                    pl.ds(summed_row(core_shift, i, p), TOKENS_OWN), :
                ].astype(BF16)


def last_back(blocks, near, middle, weight):
    depth, width = weight.shape
    pieces = sum(blocks, [])
    return pl.pallas_call(
        last_back_kernel,
        in_specs=[WHOLE] * (len(pieces) + 3),
        out_specs=[WHOLE] * 9,
        out_shape=[jax.ShapeDtypeStruct((TOKENS, width), BF16)]
        + [jax.ShapeDtypeStruct((TOKENS_Z, depth), BF16)] * 8,
        scratch_shapes=[pltpu.VMEM((TOKENS, depth), F32)],
        **settings(weight, 16),
    )(*pieces, near, middle, weight)


def gelu_tanh(value):
    return jax.nn.gelu(value, approximate=True)


def add(*values):
    total = values[0].astype(F32)
    for value in values[1:]:
        total = total + value.astype(F32)
    return total


def normalize(inputs, gain, bias):
    local = inputs.shape[1]
    local_mean = jnp.sum(inputs, axis=1) / local
    centered = inputs - local_mean[:, None]
    local_square = jnp.sum(centered * centered, axis=1)
    stats = jnp.stack([local_mean, local_square])
    every = lax.all_to_all(jnp.broadcast_to(stats[None], (NZ,) + stats.shape), "col", 0, 0)
    mean = jnp.mean(every[:, 0, :], axis=0)
    offset = every[:, 0, :] - mean[None, :]
    spread = (jnp.sum(every[:, 1, :], axis=0) + local * jnp.sum(offset * offset, axis=0)) / D
    scale = lax.rsqrt(spread + 1e-05)
    moved = centered + (local_mean - mean)[:, None]
    return (moved * scale[:, None] * gain[None, :] + bias[None, :]).astype(BF16)


def reduce_chain(parts):
    travelling = send_ring(parts[0], 1)
    for step, part in enumerate(parts[1:]):
        travelling = send_ring(add(part, travelling).astype(BF16), 2 * (step % 2) - 1)
    return travelling


def gather_chain(own, way, count):
    got = []
    for _ in range(count):
        own = send_ring(own, way)
        way = -way
        got.append(own)
    return got


def per_device(inputs, gain, bias, weight, d_act):
    normed = normalize(inputs, gain, bias)

    along_x = jnp.concatenate([normed] + [send_x(normed, s) for s in GATHER_X[1:]])
    along_y = [along_x] + [send_y(along_x, s) for s in GATHER_Y[1:]]
    weight, _ = lax.optimization_barrier((weight, along_x))
    along_y[3], weight = lax.optimization_barrier((along_y[3], stage(weight)))
    other = [send_core(v) for v in along_y]

    gathered, *first = first_pre(along_y + other, weight)
    rest = rest_pre(gathered, weight)
    three, four = halves_of(SUM_CUT[4:6], first)
    back, own, one, two, five, six = halves_of(SUM_CUT[:4] + SUM_CUT[6:], rest)
    longer = [reduce_chain([four[h], five[h], two[h], back[h]]) for h in range(2)]
    shorter = reduce_chain([three[0], six[0], one[0]])
    pre = add(own[0], jnp.concatenate(longer, axis=1), shorter)
    slopes = jax.vjp(gelu_tanh, pre)[1](d_act.astype(F32))[0].astype(BF16)

    half = weight.shape[1] // 2
    cut = lax.optimization_barrier((slopes[:, :half], slopes[:, half:]))
    longer = [gather_chain(part, 1, 4) for part in cut]
    shorter = [gather_chain(part, -1, 3) for part in cut]
    block_1, block_6, block_3, block_4 = ([chain[i] for chain in longer] for i in range(4))
    block_7, block_2, block_5 = ([chain[i] for chain in shorter] for i in range(3))
    nearest = [block_7, [slopes], block_1, block_2]
    near = some_back(nearest, weight)
    middle = some_back([block_3, block_6], weight)
    blocks = nearest + [block_3, block_4, block_5, block_6]
    slopes_all, *parts = last_back(blocks, near, middle, weight)
    pre, _ = lax.optimization_barrier((pre, block_4[0]))
    activated = gelu_tanh(pre).astype(BF16)

    d_weight = lax.dot_general(
        gathered, slopes_all, (((0,), (0,)), ((), ())), preferred_element_type=F32
    ).astype(BF16)

    sums = [add(parts[i], send_core(parts[4 + i])) for i in range(4)]
    arrived = [send_plane(sums[i].astype(BF16), SUM_FIRST[i], 1) for i in range(1, 4)]
    line = add(sums[0], *arrived)
    line, d_weight = lax.optimization_barrier((line, d_weight))
    blocks = [line[i * TOKENS_OWN : (i + 1) * TOKENS_OWN] for i in range(4)]
    arrived = [send_plane(blocks[i].astype(BF16), SUM_LAST[i], 0) for i in range(1, 4)]
    d_normed = add(blocks[0], *arrived).astype(BF16)
    return (activated, d_normed, d_weight)


def solution(mesh):
    return jax.shard_map(
        per_device,
        mesh=mesh,
        in_specs=(P("row", "col"), P("col"), P("col"), P("col", "row"), P("col", "row")),
        out_specs=(P("col", "row"), P("row", "col"), P("col", "row")),
        check_vma=False,
    )
```

```python
import jax
import jax.numpy as jnp
from jax import lax
from jax.experimental import pallas as pl
from jax.experimental.pallas import tpu as pltpu
from jax.sharding import PartitionSpec as P

D = 12288
F32, BF16 = jnp.float32, jnp.bfloat16

NX, NY, NC, NZ = 4, 4, 2, 8
GATHER_X, GATHER_Y, SUM_FIRST, SUM_LAST = (0, 1, 3, 2), (0, 1, 2, 3), (0, 3, 2, 1), (0, 3, 1, 2)
TOKENS_OWN = 16
TOKENS_Z = 64
TOKENS = 512
HALF = TOKENS // 2


def pairs_of(target):
    pairs = []
    for x in range(NX):
        for y in range(NY):
            for c in range(NC):
                for z in range(NZ):
                    source = ((x * NY + y) * NC + c) * NZ + z
                    tx, ty, tc, tz = target(x, y, c, z)
                    place = ((tx % NX) * NY + ty % NY) * NC + tc % NC
                    pairs.append((source, place * NZ + tz % NZ))
    return pairs


def send(value, target):
    return lax.ppermute(value, ("row", "col"), pairs_of(target))


def send_x(value, k):
    return send(value, lambda x, y, c, z: (x ^ k, y, c, z))


def send_y(value, k):
    return send(value, lambda x, y, c, z: (x, y ^ k, c, z))


def send_plane(value, k, x_core):
    return send(value, lambda x, y, c, z: (x ^ k, y, c, z) if c == x_core else (x, y ^ k, c, z))


def send_core(value):
    return send(value, lambda x, y, c, z: (x, y, c + 1, z))


def send_ring(value, way):
    return send(value, lambda x, y, c, z: (x, y, c, z + way * (1 - 2 * ((z + c) % 2))))


def row_of(block):
    row, col = lax.axis_index("row"), lax.axis_index("col")
    own = TOKENS_Z // TOKENS_OWN
    place = ((block // own - col) * (1 - 2 * ((row + col) % 2)) + 1 + 2 * NZ) % NZ
    return pl.multiple_of(place * TOKENS_Z + (block % own) * TOKENS_OWN, TOKENS_OWN)


def gathered_row(core_shift, i, p):
    row = lax.axis_index("row")
    x, y, c = row // (NY * NC), (row // NC) % NY, row % NC
    x, y = x ^ GATHER_X[p], y ^ GATHER_Y[i]
    return row_of((x * NY + y) * NC + (c + core_shift) % NC)


def summed_row(core_shift, i, p):
    row = lax.axis_index("row")
    x, y, c = row // (NY * NC), (row // NC) % NY, row % NC
    core = (c + core_shift) % NC
    x = x ^ jnp.where(core == 1, SUM_FIRST[i], SUM_LAST[p])
    y = y ^ jnp.where(core == 1, SUM_LAST[p], SUM_FIRST[i])
    return row_of((x * NY + y) * NC + core)


WHOLE = pl.BlockSpec(memory_space=pltpu.VMEM)
TILE = 512


def settings(weight, limit):
    depth, width = weight.shape
    return dict(
        compiler_params=pltpu.CompilerParams(vmem_limit_bytes=limit << 20),
        cost_estimate=pl.CostEstimate(
            flops=TOKENS * depth * width, bytes_accessed=depth * width * 2, transcendentals=0
        ),
    )


def stage_kernel(w_ref, out_ref, sem):
    copy = pltpu.make_async_copy(w_ref, out_ref, sem)
    copy.start()
    copy.wait()


def stage(weight):
    return pl.pallas_call(
        stage_kernel,
        in_specs=[pl.BlockSpec(memory_space=pl.ANY)],
        out_specs=WHOLE,
        out_shape=jax.ShapeDtypeStruct(weight.shape, weight.dtype),
        scratch_shapes=[pltpu.SemaphoreType.DMA],
        **settings(weight, 48),
    )(weight)


def multiply(rows, w_ref, outs):
    half = w_ref.shape[1] // 2
    for h in range(2):
        columns = slice(h * half, (h + 1) * half)
        product = jnp.dot(rows, w_ref[:, columns], preferred_element_type=F32).astype(BF16)
        for k, out in enumerate(outs):
            block = product[k * TOKENS_Z : (k + 1) * TOKENS_Z, :]
            if len(out) == 2:
                out[h][...] = block
            else:
                out[0][:, columns] = block


def halves_of(cut, refs):
    refs = list(refs)
    return [[refs.pop(0) for _ in range(1 + flag)] for flag in cut]


def shapes_of(cut, width):
    return [
        jax.ShapeDtypeStruct((TOKENS_Z, width // (1 + flag)), BF16)
        for flag in cut
        for _ in range(1 + flag)
    ]


SUM_CUT = (1, 0, 0, 1, 0, 1, 1, 0)
FIRST, REST = (4, 8), (0, 4)
GATHER_CUT = (1, 0, 0, 1, 0, 1, 1, 0)


def z_rows(start, stop):
    return slice(start * TOKENS_Z, stop * TOKENS_Z)


def first_kernel(*refs):
    pieces, w_ref, normed_ref, outs = refs[:8], refs[8], refs[9], refs[10:]
    for core_shift in range(2):
        for i in range(4):
            for p in range(4):
                rows = pl.ds(gathered_row(core_shift, i, p), TOKENS_OWN)
                normed_ref[rows, :] = pieces[core_shift * 4 + i][
                    p * TOKENS_OWN : (p + 1) * TOKENS_OWN, :
                ]
    multiply(normed_ref[z_rows(*FIRST), :], w_ref, halves_of(SUM_CUT[slice(*FIRST)], outs))


def rest_kernel(normed_ref, w_ref, *outs):
    multiply(normed_ref[z_rows(*REST), :], w_ref, halves_of(SUM_CUT[slice(*REST)], outs))


def first_pre(pieces, weight):
    depth, width = weight.shape
    shapes = shapes_of(SUM_CUT[slice(*FIRST)], width)
    return pl.pallas_call(
        first_kernel,
        in_specs=[WHOLE] * 9,
        out_specs=[WHOLE] * (1 + len(shapes)),
        out_shape=[jax.ShapeDtypeStruct((TOKENS, depth), BF16)] + shapes,
        **settings(weight, 16),
    )(*pieces, weight)


def rest_pre(normed, weight):
    shapes = shapes_of(SUM_CUT[slice(*REST)], weight.shape[1])
    return pl.pallas_call(
        rest_kernel,
        in_specs=[WHOLE] * 2,
        out_specs=[WHOLE] * len(shapes),
        out_shape=shapes,
        **settings(weight, 16),
    )(normed, weight)


def transposed_dot(rows, weight):
    return lax.dot_general(rows, weight, (((1,), (1,)), ((), ())), preferred_element_type=F32)


def fill(rows_ref, blocks):
    half = rows_ref.shape[1] // 2
    for k, block in enumerate(blocks):
        rows = slice(k * TOKENS_Z, (k + 1) * TOKENS_Z)
        if len(block) == 2:
            rows_ref[rows, :half] = block[0][...]
            rows_ref[rows, half:] = block[1][...]
        else:
            rows_ref[rows, :] = block[0][...]


def near_back_kernel(*refs):
    *pieces, w_ref, out_ref, rows_ref = refs
    fill(rows_ref, halves_of(GATHER_CUT[:4], pieces))
    rows = rows_ref[...]
    for start in range(0, w_ref.shape[0], TILE):
        part = slice(start, start + TILE)
        out_ref[:, part] = transposed_dot(rows, w_ref[part, :]).astype(out_ref.dtype)


def near_back(pieces, weight):
    return pl.pallas_call(
        near_back_kernel,
        in_specs=[WHOLE] * (len(pieces) + 1),
        out_specs=WHOLE,
        out_shape=jax.ShapeDtypeStruct((HALF, weight.shape[0]), BF16),
        scratch_shapes=[pltpu.VMEM((HALF, weight.shape[1]), BF16)],
        **settings(weight, 16),
    )(*pieces, weight)


def far_back_kernel(*refs):
    *pieces, near_ref, w_ref, slopes_ref = refs[:-9]
    outs, product = refs[-9:-1], refs[-1]
    fill(slopes_ref, halves_of(GATHER_CUT, pieces))
    product[:HALF, :] = near_ref[...].astype(F32)
    rows = slopes_ref[HALF:, :]
    for start in range(0, w_ref.shape[0], TILE):
        part = slice(start, start + TILE)
        product[HALF:, part] = transposed_dot(rows, w_ref[part, :])
    for core_shift in (1, 0):
        for i in range(4):
            for p in range(4):
                outs[core_shift * 4 + i][p * TOKENS_OWN : (p + 1) * TOKENS_OWN, :] = product[
                    pl.ds(summed_row(core_shift, i, p), TOKENS_OWN), :
                ].astype(BF16)


def far_back(pieces, near, weight):
    depth, width = weight.shape
    return pl.pallas_call(
        far_back_kernel,
        in_specs=[WHOLE] * (len(pieces) + 2),
        out_specs=[WHOLE] * 9,
        out_shape=[jax.ShapeDtypeStruct((TOKENS, width), BF16)]
        + [jax.ShapeDtypeStruct((TOKENS_Z, depth), BF16)] * 8,
        scratch_shapes=[pltpu.VMEM((TOKENS, depth), F32)],
        **settings(weight, 16),
    )(*pieces, near, weight)


def gelu_tanh(value):
    return jax.nn.gelu(value, approximate=True)


def add(*values):
    total = values[0].astype(F32)
    for value in values[1:]:
        total = total + value.astype(F32)
    return total


def normalize(inputs, gain, bias):
    local = inputs.shape[1]
    local_mean = jnp.sum(inputs, axis=1) / local
    centered = inputs - local_mean[:, None]
    local_square = jnp.sum(centered * centered, axis=1)
    stats = jnp.stack([local_mean, local_square])
    every = lax.all_to_all(jnp.broadcast_to(stats[None], (NZ,) + stats.shape), "col", 0, 0)
    mean = jnp.mean(every[:, 0, :], axis=0)
    offset = every[:, 0, :] - mean[None, :]
    spread = (jnp.sum(every[:, 1, :], axis=0) + local * jnp.sum(offset * offset, axis=0)) / D
    scale = lax.rsqrt(spread + 1e-05)
    moved = centered + (local_mean - mean)[:, None]
    return (moved * scale[:, None] * gain[None, :] + bias[None, :]).astype(BF16)


def gather_chain(own, way, count):
    got = []
    for _ in range(count):
        own = send_ring(own, way)
        way = -way
        got.append(own)
    return got


def per_device(inputs, gain, bias, weight, d_act):
    normed = normalize(inputs, gain, bias)

    along_x = jnp.concatenate([normed] + [send_x(normed, s) for s in GATHER_X[1:]])
    along_y = [along_x] + [send_y(along_x, s) for s in GATHER_Y[1:]]
    weight, _ = lax.optimization_barrier((weight, along_x))
    along_y[3], weight = lax.optimization_barrier((along_y[3], stage(weight)))
    other = [send_core(v) for v in along_y]

    gathered, *first = first_pre(along_y + other, weight)
    rest = rest_pre(gathered, weight)
    three, four, five, six = halves_of(SUM_CUT[slice(*FIRST)], first)
    back, own, one, two = halves_of(SUM_CUT[slice(*REST)], rest)
    arrived_3 = send_ring(three[0], 1)
    arrived_6 = send_ring(add(six[0], arrived_3).astype(BF16), -1)
    shorter = send_ring(add(one[0], arrived_6).astype(BF16), 1)
    longer = []
    for h in range(2):
        travelling = send_ring(four[h], 1)
        travelling = send_ring(add(five[h], travelling).astype(BF16), -1)
        travelling = send_ring(add(two[h], travelling).astype(BF16), 1)
        longer.append(send_ring(add(back[h], travelling).astype(BF16), -1))
    pre = add(own[0], jnp.concatenate(longer, axis=1), shorter)
    slopes = jax.vjp(gelu_tanh, pre)[1](d_act.astype(F32))[0].astype(BF16)

    half = weight.shape[1] // 2
    slopes, *cut = lax.optimization_barrier((slopes, slopes[:, :half], slopes[:, half:]))
    longer = [gather_chain(part, -1, 4) for part in cut]
    block_7, block_2, block_5, block_4 = ([chain[i] for chain in longer] for i in range(4))
    block_1, block_6, block_3 = ([v] for v in gather_chain(slopes, 1, 3))
    nearest = block_7 + [slopes] + block_1 + block_2
    pieces = nearest + block_3 + block_4 + block_5 + block_6
    pre, _ = lax.optimization_barrier((pre, block_4[0]))
    activated = gelu_tanh(pre).astype(BF16)

    near = near_back(nearest, weight)
    slopes_all, *parts = far_back(pieces, near, weight)
    d_weight = lax.dot_general(
        gathered, slopes_all, (((0,), (0,)), ((), ())), preferred_element_type=F32
    ).astype(BF16)

    sums = [add(parts[i], send_core(parts[4 + i])) for i in range(4)]
    arrived = [send_plane(sums[i].astype(BF16), SUM_FIRST[i], 1) for i in range(1, 4)]
    line = add(sums[0], *arrived)
    line, d_weight = lax.optimization_barrier((line, d_weight))
    blocks = [line[i * TOKENS_OWN : (i + 1) * TOKENS_OWN] for i in range(4)]
    arrived = [send_plane(blocks[i].astype(BF16), SUM_LAST[i], 0) for i in range(1, 4)]
    d_normed = add(blocks[0], *arrived).astype(BF16)
    return (activated, d_normed, d_weight)


def solution(mesh):
    return jax.shard_map(
        per_device,
        mesh=mesh,
        in_specs=(P("row", "col"), P("col"), P("col"), P("col", "row"), P("col", "row")),
        out_specs=(P("col", "row"), P("row", "col"), P("col", "row")),
        check_vma=False,
    )
```

```python
import jax
import jax.numpy as jnp
from jax import lax
from jax.experimental import pallas as pl
from jax.experimental.pallas import tpu as pltpu
from jax.sharding import PartitionSpec as P

D = 12288
F32, BF16 = jnp.float32, jnp.bfloat16

NX, NY, NC, NZ = 4, 4, 2, 8
GATHER_X, GATHER_Y, SUM_FIRST, SUM_LAST = (0, 1, 3, 2), (0, 1, 2, 3), (0, 3, 2, 1), (0, 3, 1, 2)
TOKENS_OWN = 16
TOKENS_Z = 64
TOKENS = 512


def pairs_of(target):
    pairs = []
    for x in range(NX):
        for y in range(NY):
            for c in range(NC):
                for z in range(NZ):
                    source = ((x * NY + y) * NC + c) * NZ + z
                    tx, ty, tc, tz = target(x, y, c, z)
                    place = ((tx % NX) * NY + ty % NY) * NC + tc % NC
                    pairs.append((source, place * NZ + tz % NZ))
    return pairs


def send(value, target):
    return lax.ppermute(value, ("row", "col"), pairs_of(target))


def send_x(value, k):
    return send(value, lambda x, y, c, z: (x ^ k, y, c, z))


def send_y(value, k):
    return send(value, lambda x, y, c, z: (x, y ^ k, c, z))


def send_plane(value, k, x_core):
    return send(value, lambda x, y, c, z: (x ^ k, y, c, z) if c == x_core else (x, y ^ k, c, z))


def send_core(value):
    return send(value, lambda x, y, c, z: (x, y, c + 1, z))


def send_ring(value, way):
    return send(value, lambda x, y, c, z: (x, y, c, z + way * (1 - 2 * ((z + c) % 2))))


def row_of(block):
    row, col = lax.axis_index("row"), lax.axis_index("col")
    own = TOKENS_Z // TOKENS_OWN
    place = ((block // own - col) * (1 - 2 * ((row + col) % 2)) + 1 + 2 * NZ) % NZ
    return pl.multiple_of(place * TOKENS_Z + (block % own) * TOKENS_OWN, TOKENS_OWN)


def gathered_row(core_shift, i, p):
    row = lax.axis_index("row")
    x, y, c = row // (NY * NC), (row // NC) % NY, row % NC
    x, y = x ^ GATHER_X[p], y ^ GATHER_Y[i]
    return row_of((x * NY + y) * NC + (c + core_shift) % NC)


def summed_row(core_shift, i, p):
    row = lax.axis_index("row")
    x, y, c = row // (NY * NC), (row // NC) % NY, row % NC
    core = (c + core_shift) % NC
    x = x ^ jnp.where(core == 1, SUM_FIRST[i], SUM_LAST[p])
    y = y ^ jnp.where(core == 1, SUM_LAST[p], SUM_FIRST[i])
    return row_of((x * NY + y) * NC + core)


WHOLE = pl.BlockSpec(memory_space=pltpu.VMEM)
TILE = 512


def settings(weight, limit):
    depth, width = weight.shape
    return dict(
        compiler_params=pltpu.CompilerParams(vmem_limit_bytes=limit << 20),
        cost_estimate=pl.CostEstimate(
            flops=TOKENS * depth * width, bytes_accessed=depth * width * 2, transcendentals=0
        ),
    )


def stage_kernel(w_ref, out_ref, sem):
    copy = pltpu.make_async_copy(w_ref, out_ref, sem)
    copy.start()
    copy.wait()


def stage(weight):
    return pl.pallas_call(
        stage_kernel,
        in_specs=[pl.BlockSpec(memory_space=pl.ANY)],
        out_specs=WHOLE,
        out_shape=jax.ShapeDtypeStruct(weight.shape, weight.dtype),
        scratch_shapes=[pltpu.SemaphoreType.DMA],
        **settings(weight, 48),
    )(weight)


def multiply(rows, w_ref, outs):
    half = w_ref.shape[1] // 2
    for h in range(2):
        columns = slice(h * half, (h + 1) * half)
        product = jnp.dot(rows, w_ref[:, columns], preferred_element_type=F32).astype(BF16)
        for k, out in enumerate(outs):
            block = product[k * TOKENS_Z : (k + 1) * TOKENS_Z, :]
            if len(out) == 2:
                out[h][...] = block
            else:
                out[0][:, columns] = block


def halves_of(cut, refs):
    refs = list(refs)
    return [[refs.pop(0) for _ in range(1 + flag)] for flag in cut]


def shapes_of(cut, width):
    return [
        jax.ShapeDtypeStruct((TOKENS_Z, width // (1 + flag)), BF16)
        for flag in cut
        for _ in range(1 + flag)
    ]


SUM_CUT = (1, 0, 0, 1, 0, 1, 1, 0)
FIRST, REST = (4, 8), (0, 4)


def z_rows(start, stop):
    return slice(start * TOKENS_Z, stop * TOKENS_Z)


def first_kernel(*refs):
    pieces, w_ref, normed_ref, outs = refs[:8], refs[8], refs[9], refs[10:]
    for core_shift in range(2):
        for i in range(4):
            for p in range(4):
                rows = pl.ds(gathered_row(core_shift, i, p), TOKENS_OWN)
                normed_ref[rows, :] = pieces[core_shift * 4 + i][
                    p * TOKENS_OWN : (p + 1) * TOKENS_OWN, :
                ]
    multiply(normed_ref[z_rows(*FIRST), :], w_ref, halves_of(SUM_CUT[slice(*FIRST)], outs))


def rest_kernel(normed_ref, w_ref, *outs):
    multiply(normed_ref[z_rows(*REST), :], w_ref, halves_of(SUM_CUT[slice(*REST)], outs))


def first_pre(pieces, weight):
    depth, width = weight.shape
    shapes = shapes_of(SUM_CUT[slice(*FIRST)], width)
    return pl.pallas_call(
        first_kernel,
        in_specs=[WHOLE] * 9,
        out_specs=[WHOLE] * (1 + len(shapes)),
        out_shape=[jax.ShapeDtypeStruct((TOKENS, depth), BF16)] + shapes,
        **settings(weight, 16),
    )(*pieces, weight)


def rest_pre(normed, weight):
    shapes = shapes_of(SUM_CUT[slice(*REST)], weight.shape[1])
    return pl.pallas_call(
        rest_kernel,
        in_specs=[WHOLE] * 2,
        out_specs=[WHOLE] * len(shapes),
        out_shape=shapes,
        **settings(weight, 16),
    )(normed, weight)


def transposed_dot(rows, weight):
    return lax.dot_general(rows, weight, (((1,), (1,)), ((), ())), preferred_element_type=F32)


def some_back_kernel(*refs):
    *pieces, w_ref, out_ref = refs
    rows = jnp.concatenate([piece[...] for piece in pieces], axis=0)
    for start in range(0, w_ref.shape[0], TILE):
        part = slice(start, start + TILE)
        out_ref[:, part] = transposed_dot(rows, w_ref[part, :]).astype(out_ref.dtype)


def some_back(pieces, weight):
    return pl.pallas_call(
        some_back_kernel,
        in_specs=[WHOLE] * (len(pieces) + 1),
        out_specs=WHOLE,
        out_shape=jax.ShapeDtypeStruct((len(pieces) * TOKENS_Z, weight.shape[0]), BF16),
        **settings(weight, 16),
    )(*pieces, weight)


def last_back_kernel(*refs):
    pieces, (own_ref, near_ref, w_ref, slopes_ref), outs, product = (
        refs[:8], refs[8:12], refs[12:20], refs[20]
    )
    for k, piece in enumerate(pieces):
        slopes_ref[z_rows(k, k + 1), :] = piece[...]
    product[z_rows(0, 1), :] = near_ref[z_rows(0, 1), :].astype(F32)
    product[z_rows(1, 2), :] = own_ref[...].astype(F32)
    product[z_rows(2, 4), :] = near_ref[z_rows(1, 3), :].astype(F32)
    rows = slopes_ref[z_rows(4, 8), :]
    for start in range(0, w_ref.shape[0], TILE):
        part = slice(start, start + TILE)
        product[z_rows(4, 8), part] = transposed_dot(rows, w_ref[part, :])
    for core_shift in (1, 0):
        for i in range(4):
            for p in range(4):
                outs[core_shift * 4 + i][p * TOKENS_OWN : (p + 1) * TOKENS_OWN, :] = product[
                    pl.ds(summed_row(core_shift, i, p), TOKENS_OWN), :
                ].astype(BF16)


def last_back(pieces, own, near, weight):
    depth, width = weight.shape
    return pl.pallas_call(
        last_back_kernel,
        in_specs=[WHOLE] * 11,
        out_specs=[WHOLE] * 9,
        out_shape=[jax.ShapeDtypeStruct((TOKENS, width), BF16)]
        + [jax.ShapeDtypeStruct((TOKENS_Z, depth), BF16)] * 8,
        scratch_shapes=[pltpu.VMEM((TOKENS, depth), F32)],
        **settings(weight, 16),
    )(*pieces, own, near, weight)


def gelu_tanh(value):
    return jax.nn.gelu(value, approximate=True)


def add(*values):
    total = values[0].astype(F32)
    for value in values[1:]:
        total = total + value.astype(F32)
    return total


def normalize(inputs, gain, bias):
    local = inputs.shape[1]
    local_mean = jnp.sum(inputs, axis=1) / local
    centered = inputs - local_mean[:, None]
    local_square = jnp.sum(centered * centered, axis=1)
    stats = jnp.stack([local_mean, local_square])
    every = lax.all_to_all(jnp.broadcast_to(stats[None], (NZ,) + stats.shape), "col", 0, 0)
    mean = jnp.mean(every[:, 0, :], axis=0)
    offset = every[:, 0, :] - mean[None, :]
    spread = (jnp.sum(every[:, 1, :], axis=0) + local * jnp.sum(offset * offset, axis=0)) / D
    scale = lax.rsqrt(spread + 1e-05)
    moved = centered + (local_mean - mean)[:, None]
    return (moved * scale[:, None] * gain[None, :] + bias[None, :]).astype(BF16)


def gather_chain(own, way, count):
    got = []
    for _ in range(count):
        own = send_ring(own, way)
        way = -way
        got.append(own)
    return got


def per_device(inputs, gain, bias, weight, d_act):
    normed = normalize(inputs, gain, bias)

    along_x = jnp.concatenate([normed] + [send_x(normed, s) for s in GATHER_X[1:]])
    along_y = [along_x] + [send_y(along_x, s) for s in GATHER_Y[1:]]
    weight, _ = lax.optimization_barrier((weight, along_x))
    along_y[3], weight = lax.optimization_barrier((along_y[3], stage(weight)))
    other = [send_core(v) for v in along_y]

    gathered, *first = first_pre(along_y + other, weight)
    rest = rest_pre(gathered, weight)
    three, four, five, six = halves_of(SUM_CUT[slice(*FIRST)], first)
    back, own, one, two = halves_of(SUM_CUT[slice(*REST)], rest)
    arrived_3 = send_ring(three[0], 1)
    arrived_6 = send_ring(add(six[0], arrived_3).astype(BF16), -1)
    shorter = send_ring(add(one[0], arrived_6).astype(BF16), 1)
    longer = []
    for h in range(2):
        travelling = send_ring(four[h], 1)
        travelling = send_ring(add(five[h], travelling).astype(BF16), -1)
        travelling = send_ring(add(two[h], travelling).astype(BF16), 1)
        longer.append(send_ring(add(back[h], travelling).astype(BF16), -1))
    pre = add(own[0], jnp.concatenate(longer, axis=1), shorter)
    slopes = jax.vjp(gelu_tanh, pre)[1](d_act.astype(F32))[0].astype(BF16)

    block_1, block_6, block_3, block_4 = gather_chain(slopes, 1, 4)
    pre, _ = lax.optimization_barrier((pre, slopes))
    activated = gelu_tanh(pre).astype(BF16)
    own_back = some_back([slopes], weight)
    later, _, _ = lax.optimization_barrier((slopes, activated, own_back))
    block_7, block_2, block_5 = gather_chain(later, -1, 3)
    near = some_back([block_7, block_1, block_2], weight)
    pieces = [block_7, slopes, block_1, block_2, block_3, block_4, block_5, block_6]
    slopes_all, *parts = last_back(pieces, own_back, near, weight)
    d_weight = lax.dot_general(
        gathered, slopes_all, (((0,), (0,)), ((), ())), preferred_element_type=F32
    ).astype(BF16)

    sums = [add(parts[i], send_core(parts[4 + i])) for i in range(4)]
    arrived = [send_plane(sums[i].astype(BF16), SUM_FIRST[i], 1) for i in range(1, 4)]
    line = add(sums[0], *arrived)
    line, d_weight = lax.optimization_barrier((line, d_weight))
    blocks = [line[i * TOKENS_OWN : (i + 1) * TOKENS_OWN] for i in range(4)]
    arrived = [send_plane(blocks[i].astype(BF16), SUM_LAST[i], 0) for i in range(1, 4)]
    d_normed = add(blocks[0], *arrived).astype(BF16)
    return (activated, d_normed, d_weight)


def solution(mesh):
    return jax.shard_map(
        per_device,
        mesh=mesh,
        in_specs=(P("row", "col"), P("col"), P("col"), P("col", "row"), P("col", "row")),
        out_specs=(P("col", "row"), P("row", "col"), P("col", "row")),
        check_vma=False,
    )
```

```python
import jax
import jax.numpy as jnp
from jax import lax
from jax.experimental import pallas as pl
from jax.experimental.pallas import tpu as pltpu
from jax.sharding import PartitionSpec as P

D = 12288
F32, BF16 = jnp.float32, jnp.bfloat16

NX, NY, NC, NZ = 4, 4, 2, 8
GATHER_X, GATHER_Y, SUM_FIRST, SUM_LAST = (0, 1, 3, 2), (0, 1, 2, 3), (0, 3, 2, 1), (0, 3, 1, 2)
TOKENS_OWN = 16
TOKENS_Z = 64
TOKENS = 512
HALF = TOKENS // 2


def pairs_of(target):
    pairs = []
    for x in range(NX):
        for y in range(NY):
            for c in range(NC):
                for z in range(NZ):
                    source = ((x * NY + y) * NC + c) * NZ + z
                    tx, ty, tc, tz = target(x, y, c, z)
                    place = ((tx % NX) * NY + ty % NY) * NC + tc % NC
                    pairs.append((source, place * NZ + tz % NZ))
    return pairs


def send(value, target):
    return lax.ppermute(value, ("row", "col"), pairs_of(target))


def send_x(value, k):
    return send(value, lambda x, y, c, z: (x ^ k, y, c, z))


def send_y(value, k):
    return send(value, lambda x, y, c, z: (x, y ^ k, c, z))


def send_plane(value, k, x_core):
    return send(value, lambda x, y, c, z: (x ^ k, y, c, z) if c == x_core else (x, y ^ k, c, z))


def send_core(value):
    return send(value, lambda x, y, c, z: (x, y, c + 1, z))


def send_ring(value, way):
    return send(value, lambda x, y, c, z: (x, y, c, z + way * (1 - 2 * ((z + c) % 2))))


def row_of(block):
    row, col = lax.axis_index("row"), lax.axis_index("col")
    own = TOKENS_Z // TOKENS_OWN
    place = ((block // own - col) * (1 - 2 * ((row + col) % 2)) + 1 + 2 * NZ) % NZ
    return pl.multiple_of(place * TOKENS_Z + (block % own) * TOKENS_OWN, TOKENS_OWN)


def gathered_row(core_shift, i, p):
    row = lax.axis_index("row")
    x, y, c = row // (NY * NC), (row // NC) % NY, row % NC
    x, y = x ^ GATHER_X[p], y ^ GATHER_Y[i]
    return row_of((x * NY + y) * NC + (c + core_shift) % NC)


def summed_row(core_shift, i, p):
    row = lax.axis_index("row")
    x, y, c = row // (NY * NC), (row // NC) % NY, row % NC
    core = (c + core_shift) % NC
    x = x ^ jnp.where(core == 1, SUM_FIRST[i], SUM_LAST[p])
    y = y ^ jnp.where(core == 1, SUM_LAST[p], SUM_FIRST[i])
    return row_of((x * NY + y) * NC + core)


WHOLE = pl.BlockSpec(memory_space=pltpu.VMEM)
TILE = 512


def settings(weight, limit):
    depth, width = weight.shape
    return dict(
        compiler_params=pltpu.CompilerParams(vmem_limit_bytes=limit << 20),
        cost_estimate=pl.CostEstimate(
            flops=TOKENS * depth * width, bytes_accessed=depth * width * 2, transcendentals=0
        ),
    )


def stage_kernel(w_ref, out_ref, sem):
    copy = pltpu.make_async_copy(w_ref, out_ref, sem)
    copy.start()
    copy.wait()


def stage(weight):
    return pl.pallas_call(
        stage_kernel,
        in_specs=[pl.BlockSpec(memory_space=pl.ANY)],
        out_specs=WHOLE,
        out_shape=jax.ShapeDtypeStruct(weight.shape, weight.dtype),
        scratch_shapes=[pltpu.SemaphoreType.DMA],
        **settings(weight, 48),
    )(weight)


def multiply(rows, w_ref, outs):
    half = w_ref.shape[1] // 2
    for h in range(2):
        columns = slice(h * half, (h + 1) * half)
        product = jnp.dot(rows, w_ref[:, columns], preferred_element_type=F32).astype(BF16)
        for k, out in enumerate(outs):
            block = product[k * TOKENS_Z : (k + 1) * TOKENS_Z, :]
            if len(out) == 2:
                out[h][...] = block
            else:
                out[0][:, columns] = block


def halves_of(cut, refs):
    refs = list(refs)
    return [[refs.pop(0) for _ in range(1 + flag)] for flag in cut]


def shapes_of(cut, width):
    return [
        jax.ShapeDtypeStruct((TOKENS_Z, width // (1 + flag)), BF16)
        for flag in cut
        for _ in range(1 + flag)
    ]


SUM_CUT = (1, 0, 0, 1, 0, 1, 1, 0)
FIRST, REST = (4, 8), (0, 4)
GATHER_CUT = (1, 0, 1, 1, 1, 1, 1, 1)


def z_rows(start, stop):
    return slice(start * TOKENS_Z, stop * TOKENS_Z)


def first_kernel(*refs):
    pieces, w_ref, normed_ref, outs = refs[:8], refs[8], refs[9], refs[10:]
    for core_shift in range(2):
        for i in range(4):
            for p in range(4):
                rows = pl.ds(gathered_row(core_shift, i, p), TOKENS_OWN)
                normed_ref[rows, :] = pieces[core_shift * 4 + i][
                    p * TOKENS_OWN : (p + 1) * TOKENS_OWN, :
                ]
    multiply(normed_ref[z_rows(*FIRST), :], w_ref, halves_of(SUM_CUT[slice(*FIRST)], outs))


def rest_kernel(normed_ref, w_ref, *outs):
    multiply(normed_ref[z_rows(*REST), :], w_ref, halves_of(SUM_CUT[slice(*REST)], outs))


def first_pre(pieces, weight):
    depth, width = weight.shape
    shapes = shapes_of(SUM_CUT[slice(*FIRST)], width)
    return pl.pallas_call(
        first_kernel,
        in_specs=[WHOLE] * 9,
        out_specs=[WHOLE] * (1 + len(shapes)),
        out_shape=[jax.ShapeDtypeStruct((TOKENS, depth), BF16)] + shapes,
        **settings(weight, 16),
    )(*pieces, weight)


def rest_pre(normed, weight):
    shapes = shapes_of(SUM_CUT[slice(*REST)], weight.shape[1])
    return pl.pallas_call(
        rest_kernel,
        in_specs=[WHOLE] * 2,
        out_specs=[WHOLE] * len(shapes),
        out_shape=shapes,
        **settings(weight, 16),
    )(normed, weight)


def transposed_dot(rows, weight):
    return lax.dot_general(rows, weight, (((1,), (1,)), ((), ())), preferred_element_type=F32)


def fill(rows_ref, blocks):
    half = rows_ref.shape[1] // 2
    for k, block in enumerate(blocks):
        rows = slice(k * TOKENS_Z, (k + 1) * TOKENS_Z)
        if len(block) == 2:
            rows_ref[rows, :half] = block[0][...]
            rows_ref[rows, half:] = block[1][...]
        else:
            rows_ref[rows, :] = block[0][...]


def near_back_kernel(*refs):
    *pieces, w_ref, out_ref, rows_ref = refs
    fill(rows_ref, halves_of(GATHER_CUT[:4], pieces))
    rows = rows_ref[...]
    for start in range(0, w_ref.shape[0], TILE):
        part = slice(start, start + TILE)
        out_ref[:, part] = transposed_dot(rows, w_ref[part, :]).astype(out_ref.dtype)


def near_back(pieces, weight):
    return pl.pallas_call(
        near_back_kernel,
        in_specs=[WHOLE] * (len(pieces) + 1),
        out_specs=WHOLE,
        out_shape=jax.ShapeDtypeStruct((HALF, weight.shape[0]), BF16),
        scratch_shapes=[pltpu.VMEM((HALF, weight.shape[1]), BF16)],
        **settings(weight, 16),
    )(*pieces, weight)


def far_back_kernel(*refs):
    *pieces, near_ref, w_ref, slopes_ref = refs[:-9]
    outs, product = refs[-9:-1], refs[-1]
    fill(slopes_ref, halves_of(GATHER_CUT, pieces))
    product[:HALF, :] = near_ref[...].astype(F32)
    rows = slopes_ref[HALF:, :]
    for start in range(0, w_ref.shape[0], TILE):
        part = slice(start, start + TILE)
        product[HALF:, part] = transposed_dot(rows, w_ref[part, :])
    for core_shift in (1, 0):
        for i in range(4):
            for p in range(4):
                outs[core_shift * 4 + i][p * TOKENS_OWN : (p + 1) * TOKENS_OWN, :] = product[
                    pl.ds(summed_row(core_shift, i, p), TOKENS_OWN), :
                ].astype(BF16)


def far_back(pieces, near, weight):
    depth, width = weight.shape
    return pl.pallas_call(
        far_back_kernel,
        in_specs=[WHOLE] * (len(pieces) + 2),
        out_specs=[WHOLE] * 9,
        out_shape=[jax.ShapeDtypeStruct((TOKENS, width), BF16)]
        + [jax.ShapeDtypeStruct((TOKENS_Z, depth), BF16)] * 8,
        scratch_shapes=[pltpu.VMEM((TOKENS, depth), F32)],
        **settings(weight, 16),
    )(*pieces, near, weight)


def gelu_tanh(value):
    return jax.nn.gelu(value, approximate=True)


def add(*values):
    total = values[0].astype(F32)
    for value in values[1:]:
        total = total + value.astype(F32)
    return total


def normalize(inputs, gain, bias):
    local = inputs.shape[1]
    local_mean = jnp.sum(inputs, axis=1) / local
    centered = inputs - local_mean[:, None]
    local_square = jnp.sum(centered * centered, axis=1)
    stats = jnp.stack([local_mean, local_square])
    every = lax.all_to_all(jnp.broadcast_to(stats[None], (NZ,) + stats.shape), "col", 0, 0)
    mean = jnp.mean(every[:, 0, :], axis=0)
    offset = every[:, 0, :] - mean[None, :]
    spread = (jnp.sum(every[:, 1, :], axis=0) + local * jnp.sum(offset * offset, axis=0)) / D
    scale = lax.rsqrt(spread + 1e-05)
    moved = centered + (local_mean - mean)[:, None]
    return (moved * scale[:, None] * gain[None, :] + bias[None, :]).astype(BF16)


def gather_chain(own, way, count):
    got = []
    for _ in range(count):
        own = send_ring(own, way)
        way = -way
        got.append(own)
    return got


def per_device(inputs, gain, bias, weight, d_act):
    normed = normalize(inputs, gain, bias)

    along_x = jnp.concatenate([normed] + [send_x(normed, s) for s in GATHER_X[1:]])
    along_y = [along_x] + [send_y(along_x, s) for s in GATHER_Y[1:]]
    weight, _ = lax.optimization_barrier((weight, along_x))
    along_y[3], weight = lax.optimization_barrier((along_y[3], stage(weight)))
    other = [send_core(v) for v in along_y]

    gathered, *first = first_pre(along_y + other, weight)
    rest = rest_pre(gathered, weight)
    three, four, five, six = halves_of(SUM_CUT[slice(*FIRST)], first)
    back, own, one, two = halves_of(SUM_CUT[slice(*REST)], rest)
    arrived_3 = send_ring(three[0], 1)
    arrived_6 = send_ring(add(six[0], arrived_3).astype(BF16), -1)
    shorter = send_ring(add(one[0], arrived_6).astype(BF16), 1)
    longer = []
    for h in range(2):
        travelling = send_ring(four[h], 1)
        travelling = send_ring(add(five[h], travelling).astype(BF16), -1)
        travelling = send_ring(add(two[h], travelling).astype(BF16), 1)
        longer.append(send_ring(add(back[h], travelling).astype(BF16), -1))
    pre = add(own[0], jnp.concatenate(longer, axis=1), shorter)
    slopes = jax.vjp(gelu_tanh, pre)[1](d_act.astype(F32))[0].astype(BF16)

    half = weight.shape[1] // 2
    cut = lax.optimization_barrier((slopes[:, :half], slopes[:, half:]))
    longer = [gather_chain(part, 1, 4) for part in cut]
    shorter = [gather_chain(part, -1, 3) for part in cut]
    block_1, block_6, block_3, block_4 = ([chain[i] for chain in longer] for i in range(4))
    block_7, block_2, block_5 = ([chain[i] for chain in shorter] for i in range(3))
    after, _ = lax.optimization_barrier((block_2[1], block_3[1]))
    nearest = block_7 + [slopes] + block_1 + [block_2[0], after]
    pieces = block_7 + [slopes] + block_1 + block_2 + block_3 + block_4 + block_5 + block_6
    pre, _ = lax.optimization_barrier((pre, block_4[0]))
    activated = gelu_tanh(pre).astype(BF16)

    near = near_back(nearest, weight)
    slopes_all, *parts = far_back(pieces, near, weight)
    d_weight = lax.dot_general(
        gathered, slopes_all, (((0,), (0,)), ((), ())), preferred_element_type=F32
    ).astype(BF16)

    sums = [add(parts[i], send_core(parts[4 + i])) for i in range(4)]
    arrived = [send_plane(sums[i].astype(BF16), SUM_FIRST[i], 1) for i in range(1, 4)]
    line = add(sums[0], *arrived)
    line, d_weight = lax.optimization_barrier((line, d_weight))
    blocks = [line[i * TOKENS_OWN : (i + 1) * TOKENS_OWN] for i in range(4)]
    arrived = [send_plane(blocks[i].astype(BF16), SUM_LAST[i], 0) for i in range(1, 4)]
    d_normed = add(blocks[0], *arrived).astype(BF16)
    return (activated, d_normed, d_weight)


def solution(mesh):
    return jax.shard_map(
        per_device,
        mesh=mesh,
        in_specs=(P("row", "col"), P("col"), P("col"), P("col", "row"), P("col", "row")),
        out_specs=(P("col", "row"), P("row", "col"), P("col", "row")),
        check_vma=False,
    )
```

```python
import jax
import jax.numpy as jnp
from jax import lax
from jax.experimental import pallas as pl
from jax.experimental.pallas import tpu as pltpu
from jax.sharding import PartitionSpec as P

D = 12288
F32, BF16 = jnp.float32, jnp.bfloat16

NX, NY, NC, NZ = 4, 4, 2, 8
GATHER_X, GATHER_Y, SUM_FIRST, SUM_LAST = (0, 1, 3, 2), (0, 1, 2, 3), (0, 3, 2, 1), (0, 3, 1, 2)
TOKENS_OWN = 16
TOKENS_Z = 64
TOKENS = 512
HALF = TOKENS // 2


def pairs_of(target):
    pairs = []
    for x in range(NX):
        for y in range(NY):
            for c in range(NC):
                for z in range(NZ):
                    source = ((x * NY + y) * NC + c) * NZ + z
                    tx, ty, tc, tz = target(x, y, c, z)
                    place = ((tx % NX) * NY + ty % NY) * NC + tc % NC
                    pairs.append((source, place * NZ + tz % NZ))
    return pairs


def send(value, target):
    return lax.ppermute(value, ("row", "col"), pairs_of(target))


def send_x(value, k):
    return send(value, lambda x, y, c, z: (x ^ k, y, c, z))


def send_y(value, k):
    return send(value, lambda x, y, c, z: (x, y ^ k, c, z))


def send_plane(value, k, x_core):
    return send(value, lambda x, y, c, z: (x ^ k, y, c, z) if c == x_core else (x, y ^ k, c, z))


def send_core(value):
    return send(value, lambda x, y, c, z: (x, y, c + 1, z))


def send_ring(value, way):
    return send(value, lambda x, y, c, z: (x, y, c, z + way * (1 - 2 * ((z + c) % 2))))


def row_of(block):
    row, col = lax.axis_index("row"), lax.axis_index("col")
    own = TOKENS_Z // TOKENS_OWN
    place = ((block // own - col) * (1 - 2 * ((row + col) % 2)) + 1 + 2 * NZ) % NZ
    return pl.multiple_of(place * TOKENS_Z + (block % own) * TOKENS_OWN, TOKENS_OWN)


def gathered_row(core_shift, i, p):
    row = lax.axis_index("row")
    x, y, c = row // (NY * NC), (row // NC) % NY, row % NC
    x, y = x ^ GATHER_X[p], y ^ GATHER_Y[i]
    return row_of((x * NY + y) * NC + (c + core_shift) % NC)


def summed_row(core_shift, i, p):
    row = lax.axis_index("row")
    x, y, c = row // (NY * NC), (row // NC) % NY, row % NC
    core = (c + core_shift) % NC
    x = x ^ jnp.where(core == 1, SUM_FIRST[i], SUM_LAST[p])
    y = y ^ jnp.where(core == 1, SUM_LAST[p], SUM_FIRST[i])
    return row_of((x * NY + y) * NC + core)


WHOLE = pl.BlockSpec(memory_space=pltpu.VMEM)
TILE = 512


def settings(weight, limit):
    depth, width = weight.shape
    return dict(
        compiler_params=pltpu.CompilerParams(vmem_limit_bytes=limit << 20),
        cost_estimate=pl.CostEstimate(
            flops=TOKENS * depth * width, bytes_accessed=depth * width * 2, transcendentals=0
        ),
    )


def stage_kernel(w_ref, out_ref, sem):
    copy = pltpu.make_async_copy(w_ref, out_ref, sem)
    copy.start()
    copy.wait()


def stage(weight):
    return pl.pallas_call(
        stage_kernel,
        in_specs=[pl.BlockSpec(memory_space=pl.ANY)],
        out_specs=WHOLE,
        out_shape=jax.ShapeDtypeStruct(weight.shape, weight.dtype),
        scratch_shapes=[pltpu.SemaphoreType.DMA],
        **settings(weight, 48),
    )(weight)


def multiply(rows, w_ref, outs):
    half = w_ref.shape[1] // 2
    for h in range(2):
        columns = slice(h * half, (h + 1) * half)
        product = jnp.dot(rows, w_ref[:, columns], preferred_element_type=F32).astype(BF16)
        for k, out in enumerate(outs):
            block = product[k * TOKENS_Z : (k + 1) * TOKENS_Z, :]
            if len(out) == 2:
                out[h][...] = block
            else:
                out[0][:, columns] = block


def halves_of(cut, refs):
    refs = list(refs)
    return [[refs.pop(0) for _ in range(1 + flag)] for flag in cut]


def shapes_of(cut, width):
    return [
        jax.ShapeDtypeStruct((TOKENS_Z, width // (1 + flag)), BF16)
        for flag in cut
        for _ in range(1 + flag)
    ]


SUM_CUT = (1, 0, 0, 1, 0, 1, 1, 0)
FIRST, REST = (4, 6), (0, 4, 6, 8)
GATHER_CUT = (1, 0, 1, 1, 1, 1, 1, 1)


def z_rows(start, stop):
    return slice(start * TOKENS_Z, stop * TOKENS_Z)


def first_kernel(*refs):
    pieces, w_ref, normed_ref, outs = refs[:8], refs[8], refs[9], refs[10:]
    for core_shift in range(2):
        for i in range(4):
            for p in range(4):
                rows = pl.ds(gathered_row(core_shift, i, p), TOKENS_OWN)
                normed_ref[rows, :] = pieces[core_shift * 4 + i][
                    p * TOKENS_OWN : (p + 1) * TOKENS_OWN, :
                ]
    multiply(normed_ref[z_rows(*FIRST), :], w_ref, halves_of(SUM_CUT[slice(*FIRST)], outs))


def rest_kernel(normed_ref, w_ref, *outs):
    outs = list(outs)
    for part in (REST[:2], REST[2:]):
        cut = SUM_CUT[slice(*part)]
        count = len(cut) + sum(cut)
        multiply(normed_ref[z_rows(*part), :], w_ref, halves_of(cut, outs[:count]))
        outs = outs[count:]


def first_pre(pieces, weight):
    depth, width = weight.shape
    shapes = shapes_of(SUM_CUT[slice(*FIRST)], width)
    return pl.pallas_call(
        first_kernel,
        in_specs=[WHOLE] * 9,
        out_specs=[WHOLE] * (1 + len(shapes)),
        out_shape=[jax.ShapeDtypeStruct((TOKENS, depth), BF16)] + shapes,
        **settings(weight, 16),
    )(*pieces, weight)


def rest_pre(normed, weight):
    shapes = shapes_of(SUM_CUT[slice(*REST[:2])] + SUM_CUT[slice(*REST[2:])], weight.shape[1])
    return pl.pallas_call(
        rest_kernel,
        in_specs=[WHOLE] * 2,
        out_specs=[WHOLE] * len(shapes),
        out_shape=shapes,
        **settings(weight, 16),
    )(normed, weight)


def transposed_dot(rows, weight):
    return lax.dot_general(rows, weight, (((1,), (1,)), ((), ())), preferred_element_type=F32)


def fill(rows_ref, blocks):
    half = rows_ref.shape[1] // 2
    for k, block in enumerate(blocks):
        rows = slice(k * TOKENS_Z, (k + 1) * TOKENS_Z)
        if len(block) == 2:
            rows_ref[rows, :half] = block[0][...]
            rows_ref[rows, half:] = block[1][...]
        else:
            rows_ref[rows, :] = block[0][...]


def near_back_kernel(*refs):
    *pieces, w_ref, out_ref, rows_ref = refs
    fill(rows_ref, halves_of(GATHER_CUT[:4], pieces))
    rows = rows_ref[...]
    for start in range(0, w_ref.shape[0], TILE):
        part = slice(start, start + TILE)
        out_ref[:, part] = transposed_dot(rows, w_ref[part, :]).astype(out_ref.dtype)


def near_back(pieces, weight):
    return pl.pallas_call(
        near_back_kernel,
        in_specs=[WHOLE] * (len(pieces) + 1),
        out_specs=[WHOLE] * 2,
        out_shape=[jax.ShapeDtypeStruct((HALF, width), BF16) for width in weight.shape],
        **settings(weight, 16),
    )(*pieces, weight)


def far_back_kernel(*refs):
    *pieces, near_ref, w_ref, slopes_ref = refs[:-9]
    outs, product = refs[-9:-1], refs[-1]
    fill(slopes_ref, halves_of(GATHER_CUT[4:], pieces))
    product[:HALF, :] = near_ref[...]
    rows = slopes_ref[...]
    for start in range(0, w_ref.shape[0], TILE):
        part = slice(start, start + TILE)
        product[HALF:, part] = transposed_dot(rows, w_ref[part, :]).astype(BF16)
    for core_shift in (1, 0):
        for i in range(4):
            for p in range(4):
                outs[core_shift * 4 + i][p * TOKENS_OWN : (p + 1) * TOKENS_OWN, :] = product[
                    pl.ds(summed_row(core_shift, i, p), TOKENS_OWN), :
                ]


def far_back(pieces, near, weight):
    depth, width = weight.shape
    return pl.pallas_call(
        far_back_kernel,
        in_specs=[WHOLE] * (len(pieces) + 2),
        out_specs=[WHOLE] * 9,
        out_shape=[jax.ShapeDtypeStruct((HALF, width), BF16)]
        + [jax.ShapeDtypeStruct((TOKENS_Z, depth), BF16)] * 8,
        scratch_shapes=[pltpu.VMEM((TOKENS, depth), BF16)],
        **settings(weight, 16),
    )(*pieces, near, weight)


def gelu_tanh(value):
    return jax.nn.gelu(value, approximate=True)


def add(*values):
    total = values[0].astype(F32)
    for value in values[1:]:
        total = total + value.astype(F32)
    return total


def normalize(inputs, gain, bias):
    local = inputs.shape[1]
    local_mean = jnp.sum(inputs, axis=1) / local
    centered = inputs - local_mean[:, None]
    local_square = jnp.sum(centered * centered, axis=1)
    stats = jnp.stack([local_mean, local_square])
    every = lax.all_to_all(jnp.broadcast_to(stats[None], (NZ,) + stats.shape), "col", 0, 0)
    mean = jnp.mean(every[:, 0, :], axis=0)
    offset = every[:, 0, :] - mean[None, :]
    spread = (jnp.sum(every[:, 1, :], axis=0) + local * jnp.sum(offset * offset, axis=0)) / D
    scale = lax.rsqrt(spread + 1e-05)
    moved = centered + (local_mean - mean)[:, None]
    return (moved * scale[:, None] * gain[None, :] + bias[None, :]).astype(BF16)


def gather_chain(own, way, count):
    got = []
    for _ in range(count):
        own = send_ring(own, way)
        way = -way
        got.append(own)
    return got


def per_device(inputs, gain, bias, weight, d_act):
    normed = normalize(inputs, gain, bias)

    along_x = jnp.concatenate([normed] + [send_x(normed, s) for s in GATHER_X[1:]])
    along_y = [along_x] + [send_y(along_x, s) for s in GATHER_Y[1:]]
    weight, _ = lax.optimization_barrier((weight, along_x))
    along_y[3], weight = lax.optimization_barrier((along_y[3], stage(weight)))
    other = [send_core(v) for v in along_y]

    gathered, *first = first_pre(along_y + other, weight)
    rest = rest_pre(gathered, weight)
    three, four = halves_of(SUM_CUT[4:6], first)
    back, own, one, two, five, six = halves_of(SUM_CUT[:4] + SUM_CUT[6:], rest)
    arrived_3 = send_ring(three[0], 1)
    sum_6 = add(six[0], arrived_3).astype(BF16)
    arrived_6 = send_ring(sum_6, -1)
    shorter = send_ring(add(one[0], arrived_6).astype(BF16), 1)
    longer = []
    for h in range(2):
        travelling = send_ring(four[h], 1)
        travelling = send_ring(add(five[h], travelling).astype(BF16), -1)
        travelling, _ = lax.optimization_barrier((travelling, sum_6))
        travelling = send_ring(add(two[h], travelling).astype(BF16), 1)
        longer.append(send_ring(add(back[h], travelling).astype(BF16), -1))
    pre = add(own[0], jnp.concatenate(longer, axis=1), shorter)
    slopes = jax.vjp(gelu_tanh, pre)[1](d_act.astype(F32))[0].astype(BF16)

    half = weight.shape[1] // 2
    cut = lax.optimization_barrier((slopes[:, :half], slopes[:, half:]))
    longer = [gather_chain(part, 1, 4) for part in cut]
    shorter = [gather_chain(part, -1, 3) for part in cut]
    block_1, block_6, block_3, block_4 = ([chain[i] for chain in longer] for i in range(4))
    block_7, block_2, block_5 = ([chain[i] for chain in shorter] for i in range(3))
    after, _ = lax.optimization_barrier((block_2[1], block_3[1]))
    nearest = block_7 + [slopes] + block_1 + [block_2[0], after]
    farthest = block_3 + block_4 + block_5 + block_6
    pre, _ = lax.optimization_barrier((pre, block_4[0]))
    activated = gelu_tanh(pre).astype(BF16)

    near, near_slopes = near_back(nearest, weight)
    far_slopes, *parts = far_back(farthest, near, weight)
    slopes_all = jnp.concatenate([near_slopes, far_slopes])
    d_weight = lax.dot_general(
        gathered, slopes_all, (((0,), (0,)), ((), ())), preferred_element_type=F32
    ).astype(BF16)

    sums = [add(parts[i], send_core(parts[4 + i])) for i in range(4)]
    arrived = [send_plane(sums[i].astype(BF16), SUM_FIRST[i], 1) for i in range(1, 4)]
    line = add(sums[0], *arrived)
    line, d_weight = lax.optimization_barrier((line, d_weight))
    blocks = [line[i * TOKENS_OWN : (i + 1) * TOKENS_OWN] for i in range(4)]
    arrived = [send_plane(blocks[i].astype(BF16), SUM_LAST[i], 0) for i in range(1, 4)]
    d_normed = add(blocks[0], *arrived).astype(BF16)
    return (activated, d_normed, d_weight)


def solution(mesh):
    return jax.shard_map(
        per_device,
        mesh=mesh,
        in_specs=(P("row", "col"), P("col"), P("col"), P("col", "row"), P("col", "row")),
        out_specs=(P("col", "row"), P("row", "col"), P("col", "row")),
        check_vma=False,
    )
```

```python
import jax
import jax.numpy as jnp
from jax import lax
from jax.experimental import pallas as pl
from jax.experimental.pallas import tpu as pltpu
from jax.sharding import PartitionSpec as P

D = 12288
F32, BF16 = jnp.float32, jnp.bfloat16

NX, NY, NC, NZ = 4, 4, 2, 8
GATHER_X, GATHER_Y, SUM_FIRST, SUM_LAST = (0, 1, 3, 2), (0, 1, 2, 3), (0, 3, 2, 1), (0, 3, 1, 2)
TOKENS_OWN = 16
TOKENS_Z = 64
TOKENS = 512
HALF = TOKENS // 2


def pairs_of(target):
    pairs = []
    for x in range(NX):
        for y in range(NY):
            for c in range(NC):
                for z in range(NZ):
                    source = ((x * NY + y) * NC + c) * NZ + z
                    tx, ty, tc, tz = target(x, y, c, z)
                    place = ((tx % NX) * NY + ty % NY) * NC + tc % NC
                    pairs.append((source, place * NZ + tz % NZ))
    return pairs


def send(value, target):
    return lax.ppermute(value, ("row", "col"), pairs_of(target))


def send_x(value, k):
    return send(value, lambda x, y, c, z: (x ^ k, y, c, z))


def send_y(value, k):
    return send(value, lambda x, y, c, z: (x, y ^ k, c, z))


def send_plane(value, k, x_core):
    return send(value, lambda x, y, c, z: (x ^ k, y, c, z) if c == x_core else (x, y ^ k, c, z))


def send_core(value):
    return send(value, lambda x, y, c, z: (x, y, c + 1, z))


def send_ring(value, way):
    return send(value, lambda x, y, c, z: (x, y, c, z + way * (1 - 2 * ((z + c) % 2))))


def row_of(block):
    row, col = lax.axis_index("row"), lax.axis_index("col")
    own = TOKENS_Z // TOKENS_OWN
    place = ((block // own - col) * (1 - 2 * ((row + col) % 2)) + 1 + 2 * NZ) % NZ
    return pl.multiple_of(place * TOKENS_Z + (block % own) * TOKENS_OWN, TOKENS_OWN)


def gathered_row(core_shift, i, p):
    row = lax.axis_index("row")
    x, y, c = row // (NY * NC), (row // NC) % NY, row % NC
    x, y = x ^ GATHER_X[p], y ^ GATHER_Y[i]
    return row_of((x * NY + y) * NC + (c + core_shift) % NC)


def summed_row(core_shift, i, p):
    row = lax.axis_index("row")
    x, y, c = row // (NY * NC), (row // NC) % NY, row % NC
    core = (c + core_shift) % NC
    x = x ^ jnp.where(core == 1, SUM_FIRST[i], SUM_LAST[p])
    y = y ^ jnp.where(core == 1, SUM_LAST[p], SUM_FIRST[i])
    return row_of((x * NY + y) * NC + core)


WHOLE = pl.BlockSpec(memory_space=pltpu.VMEM)
TILE = 512


def settings(weight, limit):
    depth, width = weight.shape
    return dict(
        compiler_params=pltpu.CompilerParams(vmem_limit_bytes=limit << 20),
        cost_estimate=pl.CostEstimate(
            flops=TOKENS * depth * width, bytes_accessed=depth * width * 2, transcendentals=0
        ),
    )


def stage_kernel(w_ref, out_ref, sem):
    copy = pltpu.make_async_copy(w_ref, out_ref, sem)
    copy.start()
    copy.wait()


def stage(weight):
    return pl.pallas_call(
        stage_kernel,
        in_specs=[pl.BlockSpec(memory_space=pl.ANY)],
        out_specs=WHOLE,
        out_shape=jax.ShapeDtypeStruct(weight.shape, weight.dtype),
        scratch_shapes=[pltpu.SemaphoreType.DMA],
        **settings(weight, 48),
    )(weight)


def multiply(rows, w_ref, outs):
    half = w_ref.shape[1] // 2
    for h in range(2):
        columns = slice(h * half, (h + 1) * half)
        product = jnp.dot(rows, w_ref[:, columns], preferred_element_type=F32).astype(BF16)
        for k, out in enumerate(outs):
            block = product[k * TOKENS_Z : (k + 1) * TOKENS_Z, :]
            if len(out) == 2:
                out[h][...] = block
            else:
                out[0][:, columns] = block


def halves_of(cut, refs):
    refs = list(refs)
    return [[refs.pop(0) for _ in range(1 + flag)] for flag in cut]


def shapes_of(cut, width):
    return [
        jax.ShapeDtypeStruct((TOKENS_Z, width // (1 + flag)), BF16)
        for flag in cut
        for _ in range(1 + flag)
    ]


SUM_CUT = (1, 0, 0, 1, 0, 1, 1, 0)
FIRST, REST = (4, 6), (0, 4, 6, 8)
GATHER_CUT = (1, 1, 1, 1, 1, 1, 1, 1)


def z_rows(start, stop):
    return slice(start * TOKENS_Z, stop * TOKENS_Z)


def first_kernel(*refs):
    pieces, w_ref, normed_ref, outs = refs[:8], refs[8], refs[9], refs[10:]
    for core_shift in range(2):
        for i in range(4):
            for p in range(4):
                rows = pl.ds(gathered_row(core_shift, i, p), TOKENS_OWN)
                normed_ref[rows, :] = pieces[core_shift * 4 + i][
                    p * TOKENS_OWN : (p + 1) * TOKENS_OWN, :
                ]
    multiply(normed_ref[z_rows(*FIRST), :], w_ref, halves_of(SUM_CUT[slice(*FIRST)], outs))


def rest_kernel(normed_ref, w_ref, *outs):
    outs = list(outs)
    for part in (REST[:2], REST[2:]):
        cut = SUM_CUT[slice(*part)]
        count = len(cut) + sum(cut)
        multiply(normed_ref[z_rows(*part), :], w_ref, halves_of(cut, outs[:count]))
        outs = outs[count:]


def first_pre(pieces, weight):
    depth, width = weight.shape
    shapes = shapes_of(SUM_CUT[slice(*FIRST)], width)
    return pl.pallas_call(
        first_kernel,
        in_specs=[WHOLE] * 9,
        out_specs=[WHOLE] * (1 + len(shapes)),
        out_shape=[jax.ShapeDtypeStruct((TOKENS, depth), BF16)] + shapes,
        **settings(weight, 16),
    )(*pieces, weight)


def rest_pre(normed, weight):
    shapes = shapes_of(SUM_CUT[slice(*REST[:2])] + SUM_CUT[slice(*REST[2:])], weight.shape[1])
    return pl.pallas_call(
        rest_kernel,
        in_specs=[WHOLE] * 2,
        out_specs=[WHOLE] * len(shapes),
        out_shape=shapes,
        **settings(weight, 16),
    )(normed, weight)


def transposed_dot(rows, weight):
    return lax.dot_general(rows, weight, (((1,), (1,)), ((), ())), preferred_element_type=F32)


def fill(rows_ref, blocks):
    half = rows_ref.shape[1] // 2
    for k, block in enumerate(blocks):
        rows = slice(k * TOKENS_Z, (k + 1) * TOKENS_Z)
        if len(block) == 2:
            rows_ref[rows, :half] = block[0][...]
            rows_ref[rows, half:] = block[1][...]
        else:
            rows_ref[rows, :] = block[0][...]


def near_back_kernel(*refs):
    *pieces, w_ref, out_ref, rows_ref = refs
    fill(rows_ref, halves_of(GATHER_CUT[:4], pieces))
    rows = rows_ref[...]
    for start in range(0, w_ref.shape[0], TILE):
        part = slice(start, start + TILE)
        out_ref[:, part] = transposed_dot(rows, w_ref[part, :]).astype(out_ref.dtype)


def near_back(pieces, weight):
    return pl.pallas_call(
        near_back_kernel,
        in_specs=[WHOLE] * (len(pieces) + 1),
        out_specs=[WHOLE] * 2,
        out_shape=[jax.ShapeDtypeStruct((HALF, width), BF16) for width in weight.shape],
        **settings(weight, 16),
    )(*pieces, weight)


def far_back_kernel(*refs):
    *pieces, near_ref, w_ref, slopes_ref = refs[:-9]
    outs, product = refs[-9:-1], refs[-1]
    fill(slopes_ref, halves_of(GATHER_CUT[4:], pieces))
    product[:HALF, :] = near_ref[...]
    rows = slopes_ref[...]
    for start in range(0, w_ref.shape[0], TILE):
        part = slice(start, start + TILE)
        product[HALF:, part] = transposed_dot(rows, w_ref[part, :]).astype(BF16)
    for core_shift in (1, 0):
        for i in range(4):
            for p in range(4):
                outs[core_shift * 4 + i][p * TOKENS_OWN : (p + 1) * TOKENS_OWN, :] = product[
                    pl.ds(summed_row(core_shift, i, p), TOKENS_OWN), :
                ]


def far_back(pieces, near, weight):
    depth, width = weight.shape
    return pl.pallas_call(
        far_back_kernel,
        in_specs=[WHOLE] * (len(pieces) + 2),
        out_specs=[WHOLE] * 9,
        out_shape=[jax.ShapeDtypeStruct((HALF, width), BF16)]
        + [jax.ShapeDtypeStruct((TOKENS_Z, depth), BF16)] * 8,
        scratch_shapes=[pltpu.VMEM((TOKENS, depth), BF16)],
        **settings(weight, 16),
    )(*pieces, near, weight)


def gelu_tanh(value):
    return jax.nn.gelu(value, approximate=True)


def add(*values):
    total = values[0].astype(F32)
    for value in values[1:]:
        total = total + value.astype(F32)
    return total


def normalize(inputs, gain, bias):
    local = inputs.shape[1]
    local_mean = jnp.sum(inputs, axis=1) / local
    centered = inputs - local_mean[:, None]
    local_square = jnp.sum(centered * centered, axis=1)
    stats = jnp.stack([local_mean, local_square])
    every = lax.all_to_all(jnp.broadcast_to(stats[None], (NZ,) + stats.shape), "col", 0, 0)
    mean = jnp.mean(every[:, 0, :], axis=0)
    offset = every[:, 0, :] - mean[None, :]
    spread = (jnp.sum(every[:, 1, :], axis=0) + local * jnp.sum(offset * offset, axis=0)) / D
    scale = lax.rsqrt(spread + 1e-05)
    moved = centered + (local_mean - mean)[:, None]
    return (moved * scale[:, None] * gain[None, :] + bias[None, :]).astype(BF16)


def gather_chain(own, way, count):
    got = []
    for _ in range(count):
        own = send_ring(own, way)
        way = -way
        got.append(own)
    return got


def per_device(inputs, gain, bias, weight, d_act):
    normed = normalize(inputs, gain, bias)

    along_x = jnp.concatenate([normed] + [send_x(normed, s) for s in GATHER_X[1:]])
    along_y = [along_x] + [send_y(along_x, s) for s in GATHER_Y[1:]]
    weight, _ = lax.optimization_barrier((weight, along_x))
    along_y[3], weight = lax.optimization_barrier((along_y[3], stage(weight)))
    other = [send_core(v) for v in along_y]

    gathered, *first = first_pre(along_y + other, weight)
    rest = rest_pre(gathered, weight)
    three, four = halves_of(SUM_CUT[4:6], first)
    back, own, one, two, five, six = halves_of(SUM_CUT[:4] + SUM_CUT[6:], rest)
    arrived_3 = send_ring(three[0], 1)
    sum_6 = add(six[0], arrived_3).astype(BF16)
    arrived_6 = send_ring(sum_6, -1)
    shorter = send_ring(add(one[0], arrived_6).astype(BF16), 1)
    longer = []
    for h in range(2):
        travelling = send_ring(four[h], 1)
        travelling = send_ring(add(five[h], travelling).astype(BF16), -1)
        travelling, _ = lax.optimization_barrier((travelling, sum_6))
        travelling = send_ring(add(two[h], travelling).astype(BF16), 1)
        longer.append(send_ring(add(back[h], travelling).astype(BF16), -1))
    half = weight.shape[1] // 2

    def split(value):
        return lax.optimization_barrier((value[:, :half], value[:, half:]))

    parts_of = zip(split(own[0]), longer, split(shorter))
    pres = [add(*parts) for parts in parts_of]
    cut = [
        jax.vjp(gelu_tanh, pre)[1](cotangent.astype(F32))[0].astype(BF16)
        for pre, cotangent in zip(pres, split(d_act))
    ]
    longer = [gather_chain(part, 1, 4) for part in cut[::-1]][::-1]
    shorter = [gather_chain(part, -1, 3) for part in cut[::-1]][::-1]
    block_1, block_6, block_3, block_4 = ([chain[i] for chain in longer] for i in range(4))
    block_7, block_2, block_5 = ([chain[i] for chain in shorter] for i in range(3))
    after, _ = lax.optimization_barrier((block_2[0], block_3[0]))
    nearest = block_7 + cut + block_1 + [after, block_2[1]]
    farthest = block_3 + block_4 + block_5 + block_6
    *pres, _ = lax.optimization_barrier((*pres, block_4[0]))
    activated = jnp.concatenate([gelu_tanh(pre).astype(BF16) for pre in pres], axis=1)

    near, near_slopes = near_back(nearest, weight)
    far_slopes, *parts = far_back(farthest, near, weight)
    slopes_all = jnp.concatenate([near_slopes, far_slopes])
    d_weight = lax.dot_general(
        gathered, slopes_all, (((0,), (0,)), ((), ())), preferred_element_type=F32
    ).astype(BF16)

    sums = [add(parts[i], send_core(parts[4 + i])) for i in range(4)]
    arrived = [send_plane(sums[i].astype(BF16), SUM_FIRST[i], 1) for i in range(1, 4)]
    line = add(sums[0], *arrived)
    line, d_weight = lax.optimization_barrier((line, d_weight))
    blocks = [line[i * TOKENS_OWN : (i + 1) * TOKENS_OWN] for i in range(4)]
    arrived = [send_plane(blocks[i].astype(BF16), SUM_LAST[i], 0) for i in range(1, 4)]
    d_normed = add(blocks[0], *arrived).astype(BF16)
    return (activated, d_normed, d_weight)


def solution(mesh):
    return jax.shard_map(
        per_device,
        mesh=mesh,
        in_specs=(P("row", "col"), P("col"), P("col"), P("col", "row"), P("col", "row")),
        out_specs=(P("col", "row"), P("row", "col"), P("col", "row")),
        check_vma=False,
    )
```
